128 devices in a mesh: section: 4 (over z), chan: 32 (over x, y, core).
Axes of the slice: x: 4, y: 4, z: 4, core: 2. Of those that a mesh axis runs over, the one named last changes fastest.
Arguments:
- inputs: bfloat16 [4, 256, 4096], P(None, None, 'chan'), may hold values from -6 to 6
- labels: int32 [4, 256], replicated, may hold values from 0 to 2
- conv_weight: bfloat16 [4, 9, 64, 4096], P('section', None, None, 'chan'), may hold values from -0.25 to 0.25
- point_weight: bfloat16 [4, 4096, 4096], P('section', 'chan'), may hold values from -0.1875 to 0.1875
- head_weight: bfloat16 [4096, 3], P('chan'), may hold values from -0.09375 to 0.09375
Outputs:
- grad_point: float32 [4, 4096, 4096], P('section', 'chan')
- grad_conv: float32 [4, 9, 64, 4096], P('section', None, None, 'chan')
The draws below stay inside these ranges and needn't reach their ends.
All inputs are finite; a program needn't handle non-finite values.
Results may differ from the reference program's by a relative error of at most 0.035.
Values may be sent and summed in bfloat16 or wider, within the bound.
A program may use at most 128 MiB of HBM per device.

```python
import jax
import jax.numpy as jnp
from jax import lax

C = 4096
GW = 64
TAPS = 9
BLOCKS = 4
MICRO = 4
T_MB = 256
CLASSES = 3
LOSS_SCALE = 2048
N_CHAN = 32


def plant(drawn, rng, smallest, high):
    place = [jax.random.randint(jax.random.fold_in(rng, axis), (), 0, length) for axis, length in enumerate(drawn.shape)]
    widest = drawn.shape.index(max(drawn.shape))
    neighbour = place[:widest] + [(place[widest] + 1) % drawn.shape[widest]] + place[widest + 1:]
    return drawn.at[tuple(place)].set(smallest).at[tuple(neighbour)].set(high)


def spiked(entries, rng, source, target, parts, factor):
    owner, partner = [(jnp.arange(entries.shape[position]) // (entries.shape[position] // parts)).reshape([-1 if axis == position else 1 for axis in range(entries.ndim)]) for position in (source, target)]
    chosen = jax.random.permutation(rng, parts)[partner]
    strong = (owner == chosen) | (owner == (partner + parts // 2) % parts)
    return jnp.where(strong, factor * entries, entries)


def levels(stream_key, dims, cuts, least, high):
    def one(dim, shards_of):
        steps = jax.random.uniform(jax.random.fold_in(jax.random.fold_in(stream_key, 6), dim), (shards_of,), jnp.float32, least / len(cuts), high / len(cuts))
        return jnp.repeat(jnp.exp(steps), dims[dim] // shards_of).reshape((-1,) + (1,) * (len(dims) - dim - 1))

    factor_of = one(*cuts[0])
    for cut in cuts[1:]:
        factor_of = factor_of * one(*cut)
    return factor_of


def scatter_about(stream_key, extent, deviation, most, shards=(), dtype=jnp.bfloat16):
    loudness = levels(stream_key, extent, shards, -0.22, 0.18) if shards else 1.0
    values = jax.random.normal(stream_key, extent, jnp.float32) * deviation * loudness
    return jnp.minimum(jnp.maximum(values, -most), most).astype(dtype)


def heavy_noise(stream_key, shape, spread, bound, split, heavy, held_as=jnp.bfloat16):
    drawn = spread * jax.random.normal(stream_key, shape, jnp.float32)
    if split:
        drawn = drawn * levels(stream_key, shape, split, -0.22, 0.18)
    return jnp.clip(spiked(drawn, jax.random.fold_in(stream_key, 3), *heavy), -bound, bound).astype(held_as)


def setup_inputs(seed: int = 0) -> dict:
    key_of = jax.random.split(jax.random.key(seed), 6)
    return {
        "inputs": scatter_about(key_of[0], (MICRO, T_MB, C), 1.0, 6.0, ((2, 32),)),
        "labels": plant(jax.random.randint(key_of[1], (MICRO, T_MB), 0, CLASSES), jax.random.fold_in(key_of[1], 1), 0, CLASSES - 1).astype(jnp.int32),
        "conv_weight": scatter_about(key_of[2], (BLOCKS, TAPS, GW, C), (TAPS * GW) ** -0.5, 0.25, ((0, 4), (3, 32))),
        "point_weight": heavy_noise(key_of[3], (BLOCKS, C, C), C ** -0.5, 0.1875, ((0, 4), (1, 32)), (1, 2, 32, 2.75)),
        "head_weight": scatter_about(key_of[4], (C, CLASSES), C ** -0.5, 0.09375, ((0, 32),)),
    }


def conv_apply(field, kernel, groups):
    half = TAPS // 2
    return lax.conv_general_dilated(field[None], kernel, (1,), [(half, half)], dimension_numbers=('NWC', 'WIO', 'NWC'), feature_group_count=groups, precision=lax.Precision.HIGHEST)[0]

def turn_kernel(kernel):
    taps, width, chans = kernel.shape
    shaped = kernel.reshape(taps, width, chans // width, width)
    shaped = jnp.transpose(shaped, (0, 3, 2, 1))[::-1]
    return shaped.reshape(taps, width, chans)

def kernel_grad(field, grads, width):
    half = TAPS // 2
    steps, chans = field.shape
    padded = jnp.pad(field, ((half, half), (0, 0)))
    grads3 = grads.reshape(steps, chans // width, width)
    pieces = []
    for k in range(TAPS):
        shifted = padded[k:k + steps].reshape(steps, chans // width, width)
        pieces.append(jnp.einsum('tgi,tgo->igo', shifted, grads3).reshape(width, chans))
    return jnp.stack(pieces)

def pointwise(act, weight):
    rows = C // N_CHAN
    total = jnp.zeros((act.shape[0], C), jnp.float32)
    for j in range(N_CHAN):
        part = jnp.dot(act[:, j * rows:(j + 1) * rows], weight[j * rows:(j + 1) * rows], preferred_element_type=jnp.float32)
        rounded = lax.optimization_barrier(part.astype(jnp.bfloat16))
        total = total + rounded.astype(jnp.float32)
    return total

def reference(inputs, labels, conv_weight, point_weight, head_weight):
    groups = C // GW
    grad_point = [jnp.zeros((C, C), jnp.float32) for b in range(BLOCKS)]
    grad_conv = [jnp.zeros((TAPS, GW, C), jnp.float32) for b in range(BLOCKS)]
    head32 = head_weight.astype(jnp.float32)
    for m in range(MICRO):
        state = inputs[m]
        saved = []
        for b in range(BLOCKS):
            saved.append(state)
            conv_out = conv_apply(state.astype(jnp.float32), conv_weight[b].astype(jnp.float32), groups)
            act = (conv_out * jax.nn.sigmoid(conv_out)).astype(jnp.bfloat16)
            mixed = pointwise(act, point_weight[b])
            state = (state.astype(jnp.float32) + mixed).astype(jnp.bfloat16)
        scores = jnp.dot(state, head_weight, preferred_element_type=jnp.float32)
        onehot = (labels[m][:, None] == jnp.arange(CLASSES)[None, :]).astype(jnp.float32)
        top = (jax.nn.sigmoid(scores) - onehot) * (LOSS_SCALE / (MICRO * T_MB))
        back = jnp.dot(top, head32.T, precision=lax.Precision.HIGHEST).astype(jnp.bfloat16)
        for b in range(BLOCKS - 1, -1, -1):
            state_b = saved[b]
            conv_out = conv_apply(state_b.astype(jnp.float32), conv_weight[b].astype(jnp.float32), groups)
            sig = jax.nn.sigmoid(conv_out)
            act = (conv_out * sig).astype(jnp.bfloat16)
            act_grad = lax.dot_general(back, point_weight[b], (((1,), (1,)), ((), ())), preferred_element_type=jnp.float32)
            conv_grad = (act_grad * sig * (1.0 + conv_out * (1.0 - sig))).astype(jnp.bfloat16)
            grad_point[b] = grad_point[b] + lax.dot_general(act, back, (((0,), (0,)), ((), ())), preferred_element_type=jnp.float32)
            grad_conv[b] = grad_conv[b] + kernel_grad(state_b.astype(jnp.float32), conv_grad.astype(jnp.float32), GW)
            input_grad = conv_apply(conv_grad.astype(jnp.float32), turn_kernel(conv_weight[b].astype(jnp.float32)), groups)
            back = (back.astype(jnp.float32) + input_grad).astype(jnp.bfloat16)
    return (jnp.stack(grad_point), jnp.stack(grad_conv))
```

```python
import jax
import jax.numpy as jnp
from jax import lax
from jax.experimental import pallas as pl
from jax.experimental.pallas import tpu as pltpu
from jax.sharding import PartitionSpec as P

CLASSES = 3
LOSS_SCALE = 2048
NX, NY, NC, NZ = 4, 4, 2, 4
LIVE = 3
F32, BF16 = jnp.float32, jnp.bfloat16
HIGH = lax.Precision.HIGHEST
MESH = pl.DeviceIdType.MESH


def nn(a, b, precision=None):
    return lax.dot_general(a, b, (((1,), (0,)), ((), ())), precision=precision, preferred_element_type=F32)


def nt(a, b, precision=None):
    return lax.dot_general(a, b, (((1,), (1,)), ((), ())), precision=precision, preferred_element_type=F32)


def tn(a, b, precision=None):
    return lax.dot_general(a, b, (((0,), (0,)), ((), ())), precision=precision, preferred_element_type=F32)


def wait_bytes(ref, sem):
    pltpu.make_async_copy(ref, ref, sem).wait()


def kernel(
    inputs, labels, cw, pw, head,
    out_gp, out_gc,
    w_all, cw_all, dense, cols, conv_out, act, state, pad, cgrad,
    psend, precv, summed, r1a, r1b, s1a, s1b, r2a, r2b,
    gathered, gsend, gnear, grecv, frecv, gcsend, gcrecv,
    heads, w3h, tsend, trecv, score_own, score_in,
    send, recv, cw_sem, w_sem,
):
    steps, width = inputs.shape[1], inputs.shape[2]
    taps, group = cw.shape[1], cw.shape[2]
    half = taps // 2
    top_rows = steps // 2
    span = NY * NC * width
    rows_a, rows_b = pl.ds(0, top_rows), pl.ds(top_rows, top_rows)
    z = lax.axis_index("section")
    me = lax.axis_index("chan")
    c = lax.rem(me, NC)
    y = lax.rem(lax.div(me, NC), NY)
    x = lax.div(me, NC * NY)
    other = 1 - c
    sibling = {"chan": me + 1 - 2 * c}
    xs = [lax.rem(x + 1 + r, NX) for r in range(NX)]
    ys = [lax.rem(y + 1 + r, NY) for r in range(NY)]
    xl = [lax.rem(x + NX - 1 - r, NX) for r in range(NX)]
    yl = [lax.rem(y + NY - 1 - r, NY) for r in range(NY)]
    at_x = [{"chan": (xs[r] * NY + y) * NC + c} for r in range(NX - 1)]
    at_y = [{"chan": (x * NY + ys[r]) * NC + c} for r in range(NY - 1)]
    zs = [lax.rem(z + 1 + r, NZ) for r in range(NZ - 1)]
    up, down = {"section": zs[0]}, {"section": zs[2]}

    count = [0]
    sent = []

    def link(src, dst, device, when=None):
        n = count[0]
        count[0] += 1
        copy = pltpu.make_async_remote_copy(
            src_ref=src, dst_ref=dst, send_sem=send.at[n], recv_sem=recv.at[n],
            device_id=device, device_id_type=MESH,
        )
        sent.append((copy, when))
        return copy

    barrier = pltpu.get_barrier_semaphore()
    peers = [sibling] + at_x + at_y + [{"section": s} for s in zs]
    for peer in peers:
        pl.semaphore_signal(barrier, inc=1, device_id=peer, device_id_type=MESH)
    pl.semaphore_wait(barrier, len(peers))

    pltpu.make_async_copy(cw.at[0], cw_all.at[z], cw_sem.at[z]).start()
    for r in range(NZ - 1):
        n = count[0]
        count[0] += 1
        copy = pltpu.make_async_remote_copy(
            src_ref=cw.at[0], dst_ref=cw_all.at[z], send_sem=send.at[n], recv_sem=cw_sem.at[z],
            device_id={"section": zs[r]}, device_id_type=MESH,
        )
        copy.start()
        sent.append((copy, None))

    def w_cols(r):
        return pl.ds(pl.multiple_of(xs[r] * span, span), span)

    w_local, w_up, w_down, w_far = {}, {}, {}, {}

    def w_copy(src, b, r, device, when):
        n = count[0]
        count[0] += 1
        copy = pltpu.make_async_remote_copy(
            src_ref=src, dst_ref=w_all.at[b, :, w_cols(r)], send_sem=send.at[n], recv_sem=w_sem.at[b, r],
            device_id=device, device_id_type=MESH,
        )
        sent.append((copy, when))
        return copy

    for b in range(LIVE):
        home = z == b
        relays = [z == (b + 1) % NZ, z == (b + 3) % NZ]
        for r in range(NX):
            src = pw.at[0, :, w_cols(r)]
            w_local[b, r] = pltpu.make_async_copy(src, w_all.at[b, :, w_cols(r)], w_sem.at[b, r])
            w_up[b, r] = w_copy(src, b, r, up, home)
            w_down[b, r] = w_copy(src, b, r, down, home)
            w_far[b, r] = w_copy(
                w_all.at[b, :, w_cols(r)], b, r, [up, down][r % 2], relays[r % 2]
            )

    def w_launch(b, r):
        @pl.when(z == b)
        def _():
            w_up[b, r].start()
            w_down[b, r].start()
            w_local[b, r].start()

    def w_arrive(b, r):
        wait_bytes(w_all.at[b, :, w_cols(r)], w_sem.at[b, r])

        @pl.when(z == [(b + 1) % NZ, (b + 3) % NZ][r % 2])
        def _():
            w_far[b, r].start()

    for r in range(NX):
        w_launch(0, r)

    last = z == NZ - 1
    head_core = link(heads.at[x, y, c], heads.at[x, y, c], sibling, last)
    head_x = [link(heads.at[x, y], heads.at[x, y], at_x[r], last) for r in range(NX - 1)]
    head_y = [link(heads.at[:, y], heads.at[:, y], at_y[r], last) for r in range(NY - 1)]
    w3h_out = [link(w3h, w3h, {"section": zs[r]}, last) for r in range(NZ - 1)]

    @pl.when(last)
    def _():
        heads[x, y, c] = head[...]
        head_core.start()
        head_core.wait_recv()
        for copy in head_x:
            copy.start()
        for copy in head_x:
            copy.wait_recv()
        for copy in head_y:
            copy.start()
        for copy in head_y:
            copy.wait_recv()

        def fold(i, total):
            whole = jnp.concatenate(
                [heads[i, j, k] for j in range(NY) for k in range(NC)], axis=1
            ).astype(BF16)
            return total + nt(whole, pw[0, :, pl.ds(pl.multiple_of(i * span, span), span)])

        w3h[...] = lax.fori_loop(0, NX, fold, jnp.zeros(w3h.shape, F32))
        for copy in w3h_out:
            copy.start()

    lane = lax.broadcasted_iota(jnp.int32, (group, width), 1)
    first_group = lane < group
    edge = 8
    pad[pl.ds(0, edge), :] = jnp.zeros((edge, width), F32)
    pad[pl.ds(edge + steps, edge), :] = jnp.zeros((edge, width), F32)
    state[...] = inputs[z].astype(F32)

    def conv(b):
        wait_bytes(cw_all.at[b], cw_sem.at[b])
        for k in range(taps):
            tap = cw_all[b, k].astype(F32)
            dense[b, pl.ds(k * width, group), :] = jnp.where(first_group, tap, 0.0).astype(BF16)
            dense[b, pl.ds(k * width + group, group), :] = jnp.where(first_group, 0.0, tap).astype(BF16)
        pad[pl.ds(edge, steps), :] = state[...]
        for k in range(taps):
            cols[b, :, pl.ds(k * width, width)] = pad[pl.ds(edge + k - half, steps), :].astype(BF16)
        value = nn(cols[b], dense[b])
        conv_out[b] = value
        act[b] = (value * jax.nn.sigmoid(value)).astype(BF16)

    def piece_cols(b, xr, core):
        return jnp.concatenate(
            [
                w_all[b, :, pl.ds(pl.multiple_of(xr * span + (j * NC + core) * width, width), width)]
                for j in range(NY)
            ],
            axis=1,
        )

    def mix(b):
        to_core = [link(psend.at[b, xs[r]], precv.at[b, xs[r]], sibling) for r in range(NX)]
        a1 = [link(summed.at[b, xs[r], :, rows_a], r1a.at[b, r], at_x[r]) for r in range(NX - 1)]
        b1 = [link(summed.at[b, :, ys[r], rows_b], r1b.at[b, r], at_y[r]) for r in range(NY - 1)]
        a2 = [link(s1a.at[b, ys[r]], r2a.at[b, r], at_y[r]) for r in range(NY - 1)]
        b2 = [link(s1b.at[b, xs[r]], r2b.at[b, r], at_x[r]) for r in range(NX - 1)]
        for r in range(NX + 1):
            if r < NX:
                w_arrive(b, r)
                if b == 0:
                    w_launch(1, r)
                part = nn(act[b], piece_cols(b, xs[r], other))
                for j in range(NY):
                    psend[b, xs[r], j] = part[:, j * width : (j + 1) * width].astype(BF16)
                to_core[r].start()
            if r >= 1:
                part = nn(act[b], piece_cols(b, xs[r - 1], c))
                to_core[r - 1].wait_recv()
                for j in range(NY):
                    summed[b, xs[r - 1], j] = (
                        part[:, j * width : (j + 1) * width] + precv[b, xs[r - 1], j].astype(F32)
                    ).astype(BF16)
                if r < NX:
                    a1[r - 1].start()
        for copy in b1:
            copy.start()
        if b == 0:
            for r in range(NX):
                w_launch(2, r)
        for copy in a1:
            copy.wait_recv()
        for j in range(NY):
            total = summed[b, x, j, rows_a].astype(F32)
            for r in range(NX - 1):
                total = total + r1a[b, r, j].astype(F32)
            s1a[b, j] = total.astype(BF16)
        for copy in a2:
            copy.start()
        for copy in b1:
            copy.wait_recv()
        for i in range(NX):
            total = summed[b, i, y, rows_b].astype(F32)
            for r in range(NY - 1):
                total = total + r1b[b, r, i].astype(F32)
            s1b[b, i] = total.astype(BF16)
        for copy in b2:
            copy.start()
        for copy in a2:
            copy.wait_recv()
        total = s1a[b, y].astype(F32)
        for r in range(NY - 1):
            total = total + r2a[b, r].astype(F32)
        state[rows_a, :] = (state[rows_a, :] + total).astype(BF16).astype(F32)
        for copy in b2:
            copy.wait_recv()
        total = s1b[b, x].astype(F32)
        for r in range(NX - 1):
            total = total + r2b[b, r].astype(F32)
        state[rows_b, :] = (state[rows_b, :] + total).astype(BF16).astype(F32)

    for b in range(LIVE):
        conv(b)
        mix(b)
    conv(LIVE)

    s_core = link(score_own.at[0], score_in.at[0], sibling)
    s_x = [link(score_own.at[1], score_in.at[1 + r], at_x[r]) for r in range(NX - 1)]
    s_y = [link(score_own.at[2], score_in.at[NX + r], at_y[r]) for r in range(NY - 1)]

    @pl.when(z != NZ - 1)
    def _():
        for r in range(NZ - 1):
            @pl.when(zs[NZ - 2 - r] == NZ - 1)
            def _():
                w3h_out[r].wait_recv()

    scores = nt(head[...], state[...], HIGH) + nt(w3h[...], act[LIVE].astype(F32), HIGH)
    score_own[0] = scores
    s_core.start()
    s_core.wait_recv()
    scores = scores + score_in[0]
    score_own[1] = scores
    for copy in s_x:
        copy.start()
    for copy in s_x:
        copy.wait_recv()
    for r in range(NX - 1):
        scores = scores + score_in[1 + r]
    score_own[2] = scores
    for copy in s_y:
        copy.start()
    for copy in s_y:
        copy.wait_recv()
    for r in range(NY - 1):
        scores = scores + score_in[NX + r]
    classes = lax.broadcasted_iota(jnp.int32, scores.shape, 0)
    hot = (classes == labels[pl.ds(z, 1), :]).astype(F32)
    top = (jax.nn.sigmoid(scores) - hot) * (LOSS_SCALE / (inputs.shape[0] * steps))
    top_t = top.T
    back = nn(top_t, head[...], HIGH).astype(BF16).astype(F32)
    act_grad = nn(top_t, w3h[...], HIGH)

    def silu_grad(b, act_grad):
        value = conv_out[b]
        s = jax.nn.sigmoid(value)
        result = (act_grad * s * (1.0 + value * (1.0 - s))).astype(BF16)
        cgrad[b] = result
        return result

    def input_grad(b):
        pad[pl.ds(edge, steps), :] = cgrad[b].astype(F32)
        total = jnp.zeros((steps, width), F32)
        for k in range(taps):
            shifted = pad[pl.ds(edge - k + half, steps), :].astype(BF16)
            total = total + nt(shifted, dense[b, pl.ds(k * width, width), :])
        return total

    def conv_weight_grad(b):
        whole = tn(cols[b], cgrad[b])
        n = count[0]
        count[0] += NZ - 1
        copies = []
        for d in range(1, NZ):
            copy = pltpu.make_async_remote_copy(
                src_ref=gcsend.at[b], dst_ref=gcrecv.at[d - 1], send_sem=send.at[n + d - 1],
                recv_sem=recv.at[gc_recv + d - 1], device_id={"section": jnp.int32(b)}, device_id_type=MESH,
            )
            sent.append((copy, z == (b + d) % NZ))
            copies.append(copy)
        for k in range(taps):
            piece = jnp.where(
                first_group,
                whole[k * width : k * width + group],
                whole[k * width + group : (k + 1) * width],
            )

            @pl.when(z == b)
            def _():
                out_gc[0, k] = piece

            @pl.when(z != b)
            def _():
                gcsend[b, k] = piece.astype(BF16)

        for d in range(1, NZ):
            @pl.when(z == (b + d) % NZ)
            def _():
                copies[d - 1].start()

    gc_recv = count[0]
    count[0] += NZ - 1

    gp_recv_n = count[0]
    count[0] += 2 * NX
    far_recv_n = count[0]
    count[0] += 2 * NX

    def span_at(i):
        return pl.ds(i * span, span)

    def gather_links(b):
        own = gathered.at[b, x, y, c]
        links = {}
        links["a1"] = [
            link(own.at[rows_a], own.at[rows_a], at_y[r]) for r in range(NY - 1)
        ]
        links["b1"] = [
            link(own.at[rows_b], own.at[rows_b], at_x[r]) for r in range(NX - 1)
        ]
        group_a = gathered.at[b, x, :, c, rows_a]
        group_b = gathered.at[b, :, y, c, rows_b]
        links["a2"] = [link(group_a, group_a, at_x[r]) for r in range(NX - 1)]
        links["b2"] = [link(group_b, group_b, at_y[r]) for r in range(NY - 1)]
        ca, cb = [link(group_a, group_a, sibling)], [link(group_b, group_b, sibling)]
        for r in range(NX - 1):
            part = gathered.at[b, xl[r], :, c, rows_a]
            ca.append(link(part, part, sibling))
        for r in range(NY - 1):
            part = gathered.at[b, :, yl[r], c, rows_b]
            cb.append(link(part, part, sibling))
        links["ca"], links["cb"] = ca, cb
        return links

    def gather_start(b, links):
        gathered[b, x, y, c] = back_state[0].astype(BF16)
        for copy in links["a1"] + links["b1"]:
            copy.start()

    def gather_second(links):
        for copy in links["a1"]:
            copy.wait_recv()
        for copy in links["a2"] + links["ca"][:1]:
            copy.start()
        for copy in links["b1"]:
            copy.wait_recv()
        for copy in links["b2"] + links["cb"][:1]:
            copy.start()

    def gather_last(links):
        for r in range(NX - 1):
            links["a2"][r].wait_recv()
            links["ca"][1 + r].start()
            links["b2"][r].wait_recv()
            links["cb"][1 + r].start()
        for copy in links["ca"] + links["cb"]:
            copy.wait_recv()

    def piece_of(b, i):
        return jnp.concatenate([gathered[b, i, j, k] for j in range(NY) for k in range(NC)], axis=1)

    def act_grad_of(b):
        def step(i, total):
            return total + nt(piece_of(b, i), w_all[b, :, pl.ds(pl.multiple_of(i * span, span), span)])

        return lax.fori_loop(0, NX, step, jnp.zeros((steps, width), F32))

    def point_links(b):
        home = {"section": jnp.int32(b)}
        links = {"near": [[], []], "far": []}
        for side, near in enumerate([(b + 1) % NZ, (b + 3) % NZ]):
            for i in range(NX):
                n = count[0]
                count[0] += 1
                copy = pltpu.make_async_remote_copy(
                    src_ref=gsend.at[b, :, span_at(i)], dst_ref=grecv.at[side, :, span_at(i)],
                    send_sem=send.at[n], recv_sem=recv.at[gp_recv_n + side * NX + i],
                    device_id=home, device_id_type=MESH,
                )
                sent.append((copy, z == near))
                links["near"][side].append(copy)
        for i in range(NX):
            n = count[0]
            count[0] += 1
            side = i % 2
            copy = pltpu.make_async_remote_copy(
                src_ref=gsend.at[b, :, span_at(i)], dst_ref=frecv.at[side, i // 2],
                send_sem=send.at[n], recv_sem=recv.at[far_recv_n + i],
                device_id={"section": jnp.int32([(b + 1) % NZ, (b + 3) % NZ][side])}, device_id_type=MESH,
            )
            sent.append((copy, z == (b + 2) % NZ))
            links["far"].append(copy)
        return links

    def point_grad(b, links):
        act_t = act[b].astype(F32).T.astype(BF16)

        def chunk(i):
            return nn(act_t, piece_of(b, i))

        @pl.when(z == b)
        def _():
            for i in range(NX):
                out_gp[0, :, span_at(i)] = chunk(i)

        @pl.when(z == (b + 2) % NZ)
        def _():
            for i in range(NX):
                gsend[b, :, span_at(i)] = chunk(i).astype(BF16)
                links["far"][i].start()

        for side in range(2):
            @pl.when(z == [(b + 1) % NZ, (b + 3) % NZ][side])
            def _():
                for i in range(1 - side, NX, 2):
                    gsend[b, :, span_at(i)] = chunk(i).astype(BF16)
                    links["near"][side][i].start()
                for i in range(side, NX, 2):
                    gnear[i // 2] = chunk(i)

    def point_relay(b, links):
        for side in range(2):
            @pl.when(z == [(b + 1) % NZ, (b + 3) % NZ][side])
            def _():
                for i in range(side, NX, 2):
                    links["far"][i].wait_recv()
                    gsend[b, :, span_at(i)] = (gnear[i // 2] + frecv[side, i // 2].astype(F32)).astype(BF16)
                    links["near"][side][i].start()

    back_state = [back]
    silu_grad(LIVE, act_grad)
    back_state[0] = (back_state[0] + input_grad(LIVE)).astype(BF16).astype(F32)
    links = gather_links(LIVE - 1)
    gather_start(LIVE - 1, links)
    folded = nn(top, act[LIVE].astype(F32), HIGH)
    t_links = []
    for d in range(1, NZ):
        copy = link(tsend, trecv.at[d - 1], {"section": jnp.int32(NZ - 1)}, z == (NZ - 1 + d) % NZ)
        t_links.append(copy)
    tsend[...] = folded
    for d in range(1, NZ):
        @pl.when(z == (NZ - 1 + d) % NZ)
        def _():
            t_links[d - 1].start()

    gather_second(links)
    conv_weight_grad(LIVE)
    pending = None
    for b in range(LIVE - 1, -1, -1):
        if pending is not None:
            point_relay(*pending)
        gather_last(links)
        silu_grad(b, act_grad_of(b))
        if b > 0:
            back_state[0] = (back_state[0] + input_grad(b)).astype(BF16).astype(F32)
            links = gather_links(b - 1)
            gather_start(b - 1, links)
        p_links = point_links(b)
        point_grad(b, p_links)
        if b > 0:
            gather_second(links)
        conv_weight_grad(b)
        pending = (b, p_links)
    point_relay(*pending)

    @pl.when(last)
    def _():
        total = tsend[...]
        for d in range(1, NZ):
            t_links[d - 1].wait_recv()
            total = total + trecv[d - 1]
        total_t = total.T
        for i in range(NX):
            whole = jnp.concatenate([heads[i, j, k] for j in range(NY) for k in range(NC)], axis=1)
            out_gp[0, :, span_at(i)] = nn(total_t, whole, HIGH)

    for d in range(1, NZ):
        wait_bytes(gcrecv.at[d - 1], recv.at[gc_recv + d - 1])
    for k in range(taps):
        total = out_gc[0, k]
        for d in range(1, NZ):
            total = total + gcrecv[d - 1, k].astype(F32)
        out_gc[0, k] = total

    @pl.when(z != NZ - 1)
    def _():
        for i in range(NX):
            for side in ((1, 0) if i % 2 == 0 else (0, 1)):
                wait_bytes(grecv.at[side, :, span_at(i)], recv.at[gp_recv_n + side * NX + i])
            out_gp[0, :, span_at(i)] = (
                out_gp[0, :, span_at(i)]
                + grecv[0, :, span_at(i)].astype(F32)
                + grecv[1, :, span_at(i)].astype(F32)
            )

    for copy, when in sent:
        if when is None:
            copy.wait_send()
        else:
            pl.when(when)(copy.wait_send)
    assert count[0] <= send.shape[0], count[0]


def local(inputs, labels, conv_weight, point_weight, head_weight):
    micro, steps, width = inputs.shape
    blocks, taps, group, _ = conv_weight.shape
    all_blocks = blocks * lax.axis_size("section")
    chans = point_weight.shape[2]
    span = chans // NX
    part = width
    half = steps // 2
    head = jnp.pad(head_weight.astype(F32).T, ((0, 8 - CLASSES), (0, 0)))
    vmem = pl.BlockSpec(memory_space=pltpu.VMEM)
    V = pltpu.VMEM
    scratch = [
        V((LIVE, width, chans), BF16),
        V((all_blocks, taps, group, width), BF16),
        V((all_blocks, taps * width, width), BF16),
        V((all_blocks, steps, taps * width), BF16),
        V((all_blocks, steps, width), F32),
        V((all_blocks, steps, width), BF16),
        V((steps, width), F32),
        V((steps + 16, width), F32),
        V((all_blocks, steps, width), BF16),
        V((LIVE, NX, NY, steps, part), BF16),
        V((LIVE, NX, NY, steps, part), BF16),
        V((LIVE, NX, NY, steps, part), BF16),
        V((LIVE, NX - 1, NY, half, part), BF16),
        V((LIVE, NY - 1, NX, half, part), BF16),
        V((LIVE, NY, half, part), BF16),
        V((LIVE, NX, half, part), BF16),
        V((LIVE, NY - 1, half, part), BF16),
        V((LIVE, NX - 1, half, part), BF16),
        V((LIVE, NX, NY, NC, steps, part), BF16),
        V((LIVE, width, chans), BF16),
        V((2, width, span), F32),
        V((2, width, chans), BF16),
        V((2, 2, width, span), BF16),
        V((all_blocks, taps, group, width), BF16),
        V((NZ - 1, taps, group, width), BF16),
        V((NX, NY, NC, 8, width), F32),
        V((8, width), F32),
        V((8, width), F32),
        V((NZ - 1, 8, width), F32),
        V((3, 8, steps), F32),
        V((NX + NY - 1, 8, steps), F32),
        pltpu.SemaphoreType.DMA((320,)),
        pltpu.SemaphoreType.DMA((320,)),
        pltpu.SemaphoreType.DMA((all_blocks,)),
        pltpu.SemaphoreType.DMA((LIVE, NX)),
    ]
    return pl.pallas_call(
        kernel,
        out_shape=(
            jax.ShapeDtypeStruct(point_weight.shape, F32),
            jax.ShapeDtypeStruct(conv_weight.shape, F32),
        ),
        in_specs=[vmem] * 5,
        out_specs=(vmem, vmem),
        scratch_shapes=scratch,
        compiler_params=pltpu.CompilerParams(
            collective_id=0, has_side_effects=True, vmem_limit_bytes=58 * 1024 * 1024
        ),
    )(inputs, labels, conv_weight, point_weight, head)


def solution(mesh):
    placed = (
        P(None, None, "chan"),
        P(),
        P("section", None, None, "chan"),
        P("section", "chan", None),
        P("chan", None),
    )
    return jax.shard_map(
        local,
        mesh=mesh,
        in_specs=placed,
        out_specs=(P("section", "chan", None), P("section", None, None, "chan")),
        check_vma=False,
    )
```

```python
import jax
import jax.numpy as jnp
from jax import lax
from jax.experimental import pallas as pl
from jax.experimental.pallas import tpu as pltpu
from jax.sharding import PartitionSpec as P

CLASSES = 3
LOSS_SCALE = 2048
NX, NY, NC, NZ = 4, 4, 2, 4
LIVE = 3
SUB = 4
F32, BF16 = jnp.float32, jnp.bfloat16
HIGH = lax.Precision.HIGHEST
MESH = pl.DeviceIdType.MESH


def nn(a, b, precision=None):
    return lax.dot_general(a, b, (((1,), (0,)), ((), ())), precision=precision, preferred_element_type=F32)


def nt(a, b, precision=None):
    return lax.dot_general(a, b, (((1,), (1,)), ((), ())), precision=precision, preferred_element_type=F32)


def tn(a, b, precision=None):
    return lax.dot_general(a, b, (((0,), (0,)), ((), ())), precision=precision, preferred_element_type=F32)


def wait_bytes(ref, sem):
    pltpu.make_async_copy(ref, ref, sem).wait()


def kernel(
    inputs, labels, cw, pw, head,
    out_gp, out_gc,
    w_all, cw_all, w_last, start, dense, cols, conv_out, act, state, pad, cgrad,
    pas, par, pbs, pbr, sa, sb, r1a, r1b, s1a, s1b, r2a, r2b,
    ga, gb, gsend, crecv, gpart, ghome, gcsend, gccrecv, gcpart,
    heads, w3h, tsend, trecv, score_own, score_in,
    send, recv, gp_send, gp_recv, gc_send, gc_recv, local_sem, out_sem,
):
    steps, width = start.shape
    taps, group = cw.shape[1], cw.shape[2]
    half = taps // 2
    top_rows = steps // 2
    pair = NC * width
    span = NY * pair
    rows_a, rows_b = pl.ds(0, top_rows), pl.ds(top_rows, top_rows)
    z = lax.axis_index("section")
    me = lax.axis_index("chan")
    c = lax.rem(me, NC)
    y = lax.rem(lax.div(me, NC), NY)
    x = lax.div(me, NC * NY)
    other = 1 - c
    sibling = {"chan": me + 1 - 2 * c}
    xs = [lax.rem(x + 1 + r, NX) for r in range(NX)]
    ys = [lax.rem(y + 1 + r, NY) for r in range(NY)]
    xl = [lax.rem(x + NX - 1 - r, NX) for r in range(NX)]
    yl = [lax.rem(y + NY - 1 - r, NY) for r in range(NY)]
    at_x = [{"chan": (xs[r] * NY + y) * NC + c} for r in range(NX - 1)]
    at_y = [{"chan": (x * NY + ys[r]) * NC + c} for r in range(NY - 1)]
    zs = [lax.rem(z + 1 + r, NZ) for r in range(NZ - 1)]
    up, down = {"section": zs[0]}, {"section": zs[2]}
    last = z == NZ - 1

    def is_z(*places):
        hit = z == places[0] % NZ
        for place in places[1:]:
            hit = hit | (z == place % NZ)
        return hit

    count = [0]
    sent = []

    def number():
        count[0] += 1
        return count[0] - 1

    def remote(src, dst, send_sem, recv_sem, device):
        return pltpu.make_async_remote_copy(
            src_ref=src, dst_ref=dst, send_sem=send_sem, recv_sem=recv_sem,
            device_id=device, device_id_type=MESH,
        )

    def link(src, dst, device, when=None):
        n = number()
        copy = remote(src, dst, send.at[n], recv.at[n], device)
        sent.append((copy, when))
        return copy

    pltpu.make_async_copy(inputs.at[z], start, local_sem.at[0]).start()

    @pl.when(last)
    def _():
        pltpu.make_async_copy(pw.at[0], w_last, local_sem.at[1]).start()

    barrier = pltpu.get_barrier_semaphore()
    peers = [sibling] + at_x + at_y + [{"section": s} for s in zs]
    for peer in peers:
        pl.semaphore_signal(barrier, inc=1, device_id=peer, device_id_type=MESH)
    pl.semaphore_wait(barrier, len(peers))

    class Piece:
        def __init__(self, b, way, src, ref):
            n = number()
            self.src, self.ref, self.sem, self.b = src, ref, recv.at[n], b
            device = (up, down)[way]
            order = [b + 1, b + 2, b + 3] if way == 0 else [b + 3, b + 2, b + 1]
            self.relays = is_z(*order[:2])
            self.first = remote(src, ref, send.at[n], recv.at[n], device)
            self.next = remote(ref, ref, send.at[n], recv.at[n], device)
            sent.append((self.next, z != order[2] % NZ))

        def relay(self):
            @pl.when(self.relays)
            def _():
                wait_bytes(self.ref, self.sem)
                self.next.start()

        def ready(self):
            @pl.when(jnp.logical_not(self.relays))
            def _():
                wait_bytes(self.ref, self.sem)

    def broadcast(b):
        ways = []
        for way in range(2):
            kept = pl.ds(0, half + 1) if way == 0 else pl.ds(half + 1, taps - half - 1)
            pieces = [Piece(b, way, cw.at[0, kept], cw_all.at[b, kept])]
            if b < LIVE:
                for r in range(way, NX, 2):
                    for k in range(SUB):
                        size = span // SUB
                        at = pl.ds(pl.multiple_of(xs[r] * span + k * size, size), size)
                        pieces.append(Piece(b, way, pw.at[0, :, at], w_all.at[b, :, at]))
            ways.append(pieces)
        return [piece for both in zip(*ways) for piece in both]

    pieces = [broadcast(b) for b in range(NZ)]

    def launch(b):
        @pl.when(z == b)
        def _():
            for piece in pieces[b]:
                piece.first.start()
            for piece in pieces[b]:
                pltpu.make_async_copy(piece.src, piece.ref, piece.sem).start()

    pumped = [0] * NZ

    def pump(b, amount):
        for piece in pieces[b][pumped[b] : pumped[b] + amount]:
            piece.relay()
        pumped[b] += amount

    head_core = link(heads.at[x, y, c], heads.at[x, y, c], sibling, last)
    head_x = [link(heads.at[x, y], heads.at[x, y], at_x[r], last) for r in range(NX - 1)]
    head_y = [link(heads.at[:, y], heads.at[:, y], at_y[r], last) for r in range(NY - 1)]
    w3h_out = [link(w3h, w3h, {"section": zs[r]}, last) for r in range(NZ - 1)]

    launch(0)

    @pl.when(last)
    def _():
        heads[x, y, c] = head[...]
        head_core.start()

    pump(0, 2)

    @pl.when(last)
    def _():
        head_core.wait_recv()
        for copy in head_x:
            copy.start()

    lane = lax.broadcasted_iota(jnp.int32, (group, width), 1)
    first_group = lane < group
    edge = 8
    pad[pl.ds(0, edge), :] = jnp.zeros((edge, width), F32)
    pad[pl.ds(edge + steps, edge), :] = jnp.zeros((edge, width), F32)
    wait_bytes(start, local_sem.at[0])
    state[...] = start[...].astype(F32)

    def unfold(b):
        pad[pl.ds(edge, steps), :] = state[...]
        for k in range(taps):
            cols[b, :, pl.ds(k * width, width)] = pad[pl.ds(edge + k - half, steps), :].astype(BF16)

    def widen(b):
        for piece in pieces[b][:2]:
            piece.ready()
        for k in range(taps):
            tap = cw_all[b, k].astype(F32)
            dense[b, pl.ds(k * width, group), :] = jnp.where(first_group, tap, 0.0).astype(BF16)
            dense[b, pl.ds(k * width + group, group), :] = jnp.where(first_group, 0.0, tap).astype(BF16)

    def conv(b):
        value = nn(cols[b], dense[b])
        conv_out[b] = value
        act[b] = (value * jax.nn.sigmoid(value)).astype(BF16)

    unfold(0)
    pump(0, len(pieces[0]) // 2)

    @pl.when(last)
    def _():
        for copy in head_x:
            copy.wait_recv()
        for copy in head_y:
            copy.start()

    widen(0)
    conv(0)
    pump(0, len(pieces[0]))
    launch(1)

    def mix(b):
        ca = [link(pas.at[b, r], par.at[b, r], sibling) for r in range(NX)]
        cb = [link(pbs.at[b, r], pbr.at[b, r], sibling) for r in range(NY)]
        a1 = [link(sa.at[b, r], r1a.at[b, r], at_x[r]) for r in range(NX - 1)]
        b1 = [link(sb.at[b, r], r1b.at[b, r], at_y[r]) for r in range(NY - 1)]
        a2 = [link(s1a.at[b, r], r2a.at[b, r], at_y[r]) for r in range(NY - 1)]
        b2 = [link(s1b.at[b, r], r2b.at[b, r], at_x[r]) for r in range(NX - 1)]

        def weights(place, core):
            return jnp.concatenate(
                [
                    w_all[b, :, pl.ds(pl.multiple_of(place(j) * pair + core * width, width), width)]
                    for j in range(NY)
                ],
                axis=1,
            )

        def line_a(r):
            return lambda j: xs[r] * NY + j

        def line_b(r):
            return lambda i: i * NY + ys[r]

        for piece in pieces[b][2:]:
            piece.ready()
        for r in range(NX + 1):
            if r < NX:
                for rows, line, out, copy in ((rows_a, line_a, pas, ca), (rows_b, line_b, pbs, cb)):
                    part = nn(act[b, rows, :], weights(line(r), other))
                    for j in range(NY):
                        out[b, r, j] = part[:, j * width : (j + 1) * width].astype(BF16)
                    copy[r].start()
            if r >= 1:
                q = r - 1
                for rows, line, heard, out, copy, first in (
                    (rows_a, line_a, par, sa, ca, a1),
                    (rows_b, line_b, pbr, sb, cb, b1),
                ):
                    part = nn(act[b, rows, :], weights(line(q), c))
                    copy[q].wait_recv()
                    for j in range(NY):
                        out[b, q, j] = (
                            part[:, j * width : (j + 1) * width] + heard[b, q, j].astype(F32)
                        ).astype(BF16)
                    if q < NX - 1:
                        first[q].start()
        pump(b + 1, 8)
        kept = []
        for first, second, own, heard, out, seen, mine in (
            (a1, a2, sa, r1a, s1a, ys, y),
            (b1, b2, sb, r1b, s1b, xs, x),
        ):
            for copy in first:
                copy.wait_recv()

            def total_at(j):
                total = own[b, NX - 1, j].astype(F32)
                for q in range(NX - 1):
                    total = total + heard[b, q, j].astype(F32)
                return total

            for r in range(NX - 1):
                out[b, r] = total_at(seen[r]).astype(BF16)
                second[r].start()
            kept.append(total_at(mine))
        pump(b + 1, len(pieces[0]))
        if b + 2 < NZ:
            launch(b + 2)
        for rows, second, heard, total in ((rows_a, a2, r2a, kept[0]), (rows_b, b2, r2b, kept[1])):
            for r in range(NX - 1):
                second[r].wait_recv()
                total = total + heard[b, r].astype(F32)
            state[rows, :] = (state[rows, :] + total).astype(BF16).astype(F32)

    for b in range(LIVE):
        if b > 0:
            widen(b)
            unfold(b)
            conv(b)
        mix(b)
        if b == 0:
            @pl.when(last)
            def _():
                for copy in head_y:
                    copy.wait_recv()
                wait_bytes(w_last, local_sem.at[1])

                def fold(i, total):
                    whole = jnp.concatenate(
                        [heads[i, j, k] for j in range(NY) for k in range(NC)], axis=1
                    ).astype(BF16)
                    return total + nt(whole, w_last[:, pl.ds(pl.multiple_of(i * span, span), span)])

                w3h[...] = lax.fori_loop(0, NX, fold, jnp.zeros(w3h.shape, F32))
                for copy in w3h_out:
                    copy.start()

    widen(LIVE)
    unfold(LIVE)
    conv(LIVE)

    s_core = link(score_own.at[0], score_in.at[0], sibling)
    s_x = [link(score_own.at[1], score_in.at[1 + r], at_x[r]) for r in range(NX - 1)]
    s_y = [link(score_own.at[2], score_in.at[NX + r], at_y[r]) for r in range(NY - 1)]
    for r in range(NZ - 1):
        @pl.when(z == r)
        def _():
            w3h_out[r].wait_recv()

    scores = nt(head[...], state[...], HIGH) + nt(w3h[...], act[LIVE].astype(F32), HIGH)
    score_own[0] = scores
    s_core.start()
    s_core.wait_recv()
    scores = scores + score_in[0]
    score_own[1] = scores
    for copy in s_x:
        copy.start()
    for copy in s_x:
        copy.wait_recv()
    for r in range(NX - 1):
        scores = scores + score_in[1 + r]
    score_own[2] = scores
    for copy in s_y:
        copy.start()
    for copy in s_y:
        copy.wait_recv()
    for r in range(NY - 1):
        scores = scores + score_in[NX + r]
    classes = lax.broadcasted_iota(jnp.int32, scores.shape, 0)
    hot = (classes == labels[pl.ds(z, 1), :]).astype(F32)
    top = (jax.nn.sigmoid(scores) - hot) * (LOSS_SCALE / (NZ * steps))
    top_t = top.T
    back = nn(top_t, head[...], HIGH).astype(BF16).astype(F32)
    act_grad = nn(top_t, w3h[...], HIGH)

    def silu_grad(b, act_grad):
        value = conv_out[b]
        s = jax.nn.sigmoid(value)
        cgrad[b] = (act_grad * s * (1.0 + value * (1.0 - s))).astype(BF16)

    def input_grad(b):
        pad[pl.ds(edge, steps), :] = cgrad[b].astype(F32)
        total = jnp.zeros((steps, width), F32)
        for k in range(taps):
            shifted = pad[pl.ds(edge - k + half, steps), :].astype(BF16)
            total = total + nt(shifted, dense[b, pl.ds(k * width, width), :])
        return total

    kept_taps = [pl.ds(half + 1, taps - half - 1), pl.ds(0, half + 1)]
    starts = [1, 3]
    middles = [(2, 3), (2, 1)]

    def gc_copy(b, way):
        at = kept_taps[way]
        return remote(
            gcsend.at[b, at], gccrecv.at[b, at], gc_send.at[b, way], gc_recv.at[b, way], (up, down)[way]
        )

    def conv_weight_grad(b):
        whole = tn(cols[b], cgrad[b])
        for k in range(taps):
            piece = jnp.where(
                first_group,
                whole[k * width : k * width + group],
                whole[k * width + group : (k + 1) * width],
            )
            gcpart[b, k] = piece
            gcsend[b, k] = piece.astype(BF16)
        for way in range(2):
            @pl.when(is_z(b + starts[way]))
            def _():
                gc_copy(b, way).start()

    def conv_weight_relay(b):
        for way in range(2):
            @pl.when(is_z(*[b + m for m in middles[way]]))
            def _():
                gc_copy(b, way).wait_recv()
                at = kept_taps[way]
                gcsend[b, at] = (gcpart[b, at] + gccrecv[b, at].astype(F32)).astype(BF16)
                gc_copy(b, way).start()

    def gather_links(b):
        own_a, own_b = ga.at[b, NX - 1, NY - 1, c], gb.at[b, NY - 1, NX - 1, c]
        links = {
            "a1": [link(own_a, ga.at[b, NX - 1, r, c], at_y[r]) for r in range(NY - 1)],
            "b1": [link(own_b, gb.at[b, NY - 1, r, c], at_x[r]) for r in range(NX - 1)],
            "a2own": [link(own_a, ga.at[b, r, NY - 1, c], at_x[r]) for r in range(NX - 1)],
            "b2own": [link(own_b, gb.at[b, r, NX - 1, c], at_y[r]) for r in range(NY - 1)],
        }
        rest = pl.ds(0, NX - 1)
        line_a, line_b = ga.at[b, NX - 1, rest, c], gb.at[b, NY - 1, rest, c]
        links["a2"] = [link(line_a, ga.at[b, r, rest, c], at_x[r]) for r in range(NX - 1)]
        links["b2"] = [link(line_b, gb.at[b, r, rest, c], at_y[r]) for r in range(NY - 1)]
        links["ca"] = [link(ga.at[b, r, :, c], ga.at[b, r, :, c], sibling) for r in range(NX)]
        links["cb"] = [link(gb.at[b, r, :, c], gb.at[b, r, :, c], sibling) for r in range(NY)]
        return links

    def gather_start(b, links, back):
        ga[b, NX - 1, NY - 1, c] = back[:top_rows].astype(BF16)
        gb[b, NY - 1, NX - 1, c] = back[top_rows:].astype(BF16)
        for name in ("a1", "b1", "a2own", "b2own"):
            for copy in links[name]:
                copy.start()

    def gather_second(links):
        for p in "ab":
            for copy in links[p + "1"]:
                copy.wait_recv()
            for copy in links[p + "2"]:
                copy.start()
            links["c" + p][NX - 1].start()

    def gather_third(links):
        for r in range(NX - 1):
            for p in "ab":
                links[p + "2own"][r].wait_recv()
                links[p + "2"][r].wait_recv()
                links["c" + p][r].start()

    def pair_cols(px, py):
        return pl.ds(pl.multiple_of((px * NY + py) * pair, pair), pair)

    def act_grad_of(b, links):
        totals = [jnp.zeros((top_rows, width), F32) for _ in range(2)]
        for r in [NX - 1] + list(range(NX - 1)):
            for way, buffer in enumerate((ga, gb)):
                links[("ca", "cb")[way]][r].wait_recv()
                left = jnp.concatenate([buffer[b, r, s, k] for s in range(NY) for k in range(NC)], axis=1)
                right = jnp.concatenate(
                    [
                        w_all[b, :, pair_cols(xl[r], yl[s]) if way == 0 else pair_cols(xl[s], yl[r])]
                        for s in range(NY)
                    ],
                    axis=1,
                )
                totals[way] = totals[way] + nt(left, right)
        return jnp.concatenate(totals, axis=0)

    def gp_copy(b, r, s, device):
        return remote(gsend.at[b, r, s], crecv.at[b, r, s], gp_send.at[b, r, s], gp_recv.at[b, r, s], device)

    def point_grad(b):
        act_t = act[b].astype(F32).T.astype(BF16)
        turn = jnp.where(is_z(b + starts[0]), 2, 0)
        starter = is_z(b + starts[0], b + starts[1])
        device = {"section": jnp.where(is_z(b + starts[0]), zs[0], zs[2])}
        for slot in range(NX):
            r = lax.rem(slot + turn, NX)
            for s in range(NY):
                whole = jnp.concatenate(
                    [
                        jnp.concatenate([ga[b, r, s, k] for k in range(NC)], axis=1),
                        jnp.concatenate([gb[b, s, r, k] for k in range(NC)], axis=1),
                    ],
                    axis=0,
                )
                part = nn(act_t, whole)
                if slot < 2:
                    @pl.when(starter)
                    def _():
                        gsend[b, r, s] = part.astype(BF16)
                        gp_copy(b, r, s, device).start()

                    @pl.when(jnp.logical_not(starter))
                    def _():
                        gpart[r, s] = part
                else:
                    gpart[r, s] = part

        @pl.when(z == b)
        def _():
            ghome[...] = gpart[...]

    def point_relay(b, lo, hi):
        for j in range(lo, hi):
            for way in range(2):
                r, s = (2 if way == 0 else 0) + j // NY, j % NY

                @pl.when(is_z(*[b + m for m in middles[way]]))
                def _():
                    copy = gp_copy(b, r, s, (up, down)[way])
                    copy.wait_recv()
                    gsend[b, r, s] = (gpart[r, s] + crecv[b, r, s].astype(F32)).astype(BF16)
                    copy.start()

    silu_grad(LIVE, act_grad)
    back = (back + input_grad(LIVE)).astype(BF16).astype(F32)
    links = gather_links(LIVE - 1)
    gather_start(LIVE - 1, links, back)
    tsend[...] = nn(top, act[LIVE].astype(F32), HIGH)
    t_links = [
        link(tsend, trecv.at[d - 1], {"section": jnp.int32(NZ - 1)}, z == (NZ - 1 + d) % NZ) for d in range(1, NZ)
    ]
    for d in range(1, NZ):
        @pl.when(z == (NZ - 1 + d) % NZ)
        def _():
            t_links[d - 1].start()

    gather_second(links)
    conv_weight_grad(LIVE)
    for b in range(LIVE - 1, -1, -1):
        if b + 1 < LIVE:
            point_relay(b + 1, 0, 4)
        gather_third(links)
        conv_weight_relay(b + 1)
        if b + 1 < LIVE:
            point_relay(b + 1, 4, 8)
        silu_grad(b, act_grad_of(b, links))
        if b > 0:
            back = (back + input_grad(b)).astype(BF16).astype(F32)
            links = gather_links(b - 1)
            gather_start(b - 1, links, back)
        point_grad(b)
        if b > 0:
            gather_second(links)
        conv_weight_grad(b)
    point_relay(0, 0, 8)
    conv_weight_relay(0)

    def out_copy(r, s):
        return pltpu.make_async_copy(
            ghome.at[r, s], out_gp.at[0, :, pair_cols(xl[r], yl[s])], out_sem.at[r, s]
        )

    @pl.when(last)
    def _():
        total = tsend[...]
        for d in range(1, NZ):
            t_links[d - 1].wait_recv()
            total = total + trecv[d - 1]
        total_t = total.T
        for r in range(NX):
            for s in range(NY):
                whole = jnp.concatenate([heads[xl[r], yl[s], k] for k in range(NC)], axis=1)
                ghome[r, s] = nn(total_t, whole, HIGH)
                out_copy(r, s).start()

    for b in range(LIVE):
        @pl.when(z == b)
        def _():
            for j in range(2 * NY):
                for r, s in ((2 + j // NY, j % NY), (j // NY, j % NY)):
                    gp_copy(b, r, s, up).wait_recv()
                    ghome[r, s] = ghome[r, s] + crecv[b, r, s].astype(F32)
                    out_copy(r, s).start()

    for b in range(NZ):
        @pl.when(z == b)
        def _():
            for way in range(2):
                gc_copy(b, way).wait_recv()
            out_gc[0] = gcpart[b] + gccrecv[b].astype(F32)

    for r in range(NX):
        for s in range(NY):
            out_copy(r, s).wait()
    for copy, when in sent:
        if when is None:
            copy.wait_send()
        else:
            pl.when(when)(copy.wait_send)
    for b in range(NZ):
        @pl.when(z != b)
        def _():
            for way in range(2):
                gc_copy(b, way).wait_send()
            if b < LIVE:
                for r in range(NX):
                    for s in range(NY):
                        gp_copy(b, r, s, up).wait_send()
    assert count[0] <= send.shape[0], count[0]


def local(inputs, labels, conv_weight, point_weight, head_weight):
    steps, width = inputs.shape[1:]
    blocks, taps, group, _ = conv_weight.shape
    chans = point_weight.shape[2]
    part = steps // 2
    pair = NC * width
    head = jnp.pad(head_weight.astype(F32).T, ((0, 8 - CLASSES), (0, 0)))
    vmem = pl.BlockSpec(memory_space=pltpu.VMEM)
    hbm = pl.BlockSpec(memory_space=pl.ANY)
    V = pltpu.VMEM
    dma = pltpu.SemaphoreType.DMA
    scratch = [
        V((LIVE, width, chans), BF16),
        V((NZ, taps, group, width), BF16),
        V((width, chans), BF16),
        V((steps, width), BF16),
        V((NZ, taps * width, width), BF16),
        V((NZ, steps, taps * width), BF16),
        V((NZ, steps, width), F32),
        V((NZ, steps, width), BF16),
        V((steps, width), F32),
        V((steps + 16, width), F32),
        V((NZ, steps, width), BF16),
        V((LIVE, NX, NY, part, width), BF16),
        V((LIVE, NX, NY, part, width), BF16),
        V((LIVE, NY, NX, part, width), BF16),
        V((LIVE, NY, NX, part, width), BF16),
        V((LIVE, NX, NY, part, width), BF16),
        V((LIVE, NY, NX, part, width), BF16),
        V((LIVE, NX - 1, NY, part, width), BF16),
        V((LIVE, NY - 1, NX, part, width), BF16),
        V((LIVE, NY - 1, part, width), BF16),
        V((LIVE, NX - 1, part, width), BF16),
        V((LIVE, NY - 1, part, width), BF16),
        V((LIVE, NX - 1, part, width), BF16),
        V((LIVE, NX, NY, NC, part, width), BF16),
        V((LIVE, NY, NX, NC, part, width), BF16),
        V((LIVE, NX, NY, width, pair), BF16),
        V((LIVE, NX, NY, width, pair), BF16),
        V((NX, NY, width, pair), F32),
        V((NX, NY, width, pair), F32),
        V((NZ, taps, group, width), BF16),
        V((NZ, taps, group, width), BF16),
        V((NZ, taps, group, width), F32),
        V((NX, NY, NC, 8, width), F32),
        V((8, width), F32),
        V((8, width), F32),
        V((NZ - 1, 8, width), F32),
        V((3, 8, steps), F32),
        V((NX + NY - 1, 8, steps), F32),
        dma((320,)),
        dma((320,)),
        dma((LIVE, NX, NY)),
        dma((LIVE, NX, NY)),
        dma((NZ, 2)),
        dma((NZ, 2)),
        dma((2,)),
        dma((NX, NY)),
    ]
    return pl.pallas_call(
        kernel,
        out_shape=(
            jax.ShapeDtypeStruct(point_weight.shape, F32),
            jax.ShapeDtypeStruct(conv_weight.shape, F32),
        ),
        in_specs=[hbm, vmem, hbm, hbm, vmem],
        out_specs=(hbm, vmem),
        scratch_shapes=scratch,
        compiler_params=pltpu.CompilerParams(
            collective_id=0, has_side_effects=True, vmem_limit_bytes=58 * 1024 * 1024
        ),
    )(inputs, labels, conv_weight, point_weight, head)


def solution(mesh):
    placed = (
        P(None, None, "chan"),
        P(),
        P("section", None, None, "chan"),
        P("section", "chan", None),
        P("chan", None),
    )
    return jax.shard_map(
        local,
        mesh=mesh,
        in_specs=placed,
        out_specs=(P("section", "chan", None), P("section", None, None, "chan")),
        check_vma=False,
    )
```

```python
import functools

import jax
import jax.numpy as jnp
from jax import lax
from jax.experimental import pallas as pl
from jax.experimental.pallas import tpu as pltpu
from jax.sharding import PartitionSpec as P

CLASSES = 3
LOSS_SCALE = 2048
NX, NY, NC, NZ = 4, 4, 2, 4
LIVE = 3
SUB = 4
F32, BF16 = jnp.float32, jnp.bfloat16
HIGH = lax.Precision.HIGHEST
MESH = pl.DeviceIdType.MESH


def nn(a, b, precision=None):
    return lax.dot_general(a, b, (((1,), (0,)), ((), ())), precision=precision, preferred_element_type=F32)


def nt(a, b, precision=None):
    return lax.dot_general(a, b, (((1,), (1,)), ((), ())), precision=precision, preferred_element_type=F32)


def tn(a, b, precision=None):
    return lax.dot_general(a, b, (((0,), (0,)), ((), ())), precision=precision, preferred_element_type=F32)


def wait_bytes(ref, sem):
    pltpu.make_async_copy(ref, ref, sem).wait()


def kernel(
    inputs, labels_in, cw, pw, head_in,
    out_gp, out_gc,
    labels, head_raw, head, w_all, cw_all, w_last, start, dense, cols, conv_out, act, state, pad, cgrad,
    pas, par, pbs, pbr, sa, sb, r1a, r1b, s1a, s1b, r2a, r2b,
    ga, gb, gsend, crecv, hrecv, gpart, ghome, gcsend, gccrecv, gcpart,
    heads, w3h, tsend, trecv, score_own, score_in,
    send, recv, gp_send, gp_recv, home_gp, local_sem, out_sem,
):
    steps, width = start.shape
    taps, group = cw.shape[1], cw.shape[2]
    half = taps // 2
    top_rows = steps // 2
    pair = NC * width
    span = NY * pair
    rows_a, rows_b = pl.ds(0, top_rows), pl.ds(top_rows, top_rows)
    z = lax.axis_index("section")
    me = lax.axis_index("chan")
    c = lax.rem(me, NC)
    y = lax.rem(lax.div(me, NC), NY)
    x = lax.div(me, NC * NY)
    other = 1 - c
    sibling = {"chan": me + 1 - 2 * c}
    xs = [lax.rem(x + 1 + r, NX) for r in range(NX)]
    ys = [lax.rem(y + 1 + r, NY) for r in range(NY)]
    xl = [lax.rem(x + NX - 1 - r, NX) for r in range(NX)]
    yl = [lax.rem(y + NY - 1 - r, NY) for r in range(NY)]
    at_x = [{"chan": (xs[r] * NY + y) * NC + c} for r in range(NX - 1)]
    at_y = [{"chan": (x * NY + ys[r]) * NC + c} for r in range(NY - 1)]
    zs = [lax.rem(z + 1 + r, NZ) for r in range(NZ - 1)]
    up, down = {"section": zs[0]}, {"section": zs[2]}
    last = z == NZ - 1

    def is_z(*places):
        hit = z == places[0] % NZ
        for place in places[1:]:
            hit = hit | (z == place % NZ)
        return hit

    count = [0]

    def number():
        count[0] += 1
        return count[0] - 1

    def remote(src, dst, send_sem, recv_sem, device):
        return pltpu.make_async_remote_copy(
            src_ref=src, dst_ref=dst, send_sem=send_sem, recv_sem=recv_sem,
            device_id=device, device_id_type=MESH,
        )

    sends = [0]
    drains = []

    def lane_of(total, when=None):
        sends[0] += 1
        sem = send.at[sends[0] - 1]
        drains.append((total, sem, when))
        return sem

    def fan(copies, total, when=None):
        sem = lane_of(total, when)
        return [remote(src, dst, sem, recv.at[number()], device) for src, dst, device in copies]

    def link(src, dst, device, when=None):
        return fan([(src, dst, device)], src, when)[0]

    pltpu.make_async_copy(inputs.at[z], start, local_sem.at[0]).start()
    pltpu.make_async_copy(labels_in, labels, local_sem.at[2]).start()
    pltpu.make_async_copy(head_in, head_raw, local_sem.at[3]).start()

    @pl.when(last)
    def _():
        pltpu.make_async_copy(pw.at[0], w_last, local_sem.at[1]).start()

    barrier = pltpu.get_barrier_semaphore()
    peers = [sibling] + at_x + at_y + [{"section": s} for s in zs]
    for peer in peers:
        pl.semaphore_signal(barrier, inc=1, device_id=peer, device_id_type=MESH)
    pl.semaphore_wait(barrier, len(peers))

    class Piece:
        def __init__(self, b, way, src, ref, sem):
            self.src, self.ref, self.sem = src, ref, recv.at[number()]
            device = (up, down)[way]
            self.order = [b + 1, b + 2, b + 3] if way == 0 else [b + 3, b + 2, b + 1]
            self.first = remote(src, ref, sem, self.sem, device)
            self.next = remote(ref, ref, sem, self.sem, device)

        def relay(self, hop):
            @pl.when(is_z(self.order[hop]))
            def _():
                wait_bytes(self.ref, self.sem)
                self.next.start()

        def ready(self):
            @pl.when(jnp.logical_not(is_z(*self.order[:2])))
            def _():
                wait_bytes(self.ref, self.sem)

    taps_of, columns_of = [], []
    for b in range(NZ):
        for way in range(2):
            end = z != (b + (3, 1)[way]) % NZ
            kept = pl.ds(0, half + 1) if way == 0 else pl.ds(half + 1, taps - half - 1)
            ref = cw_all.at[b, kept]
            taps_of.append(Piece(b, way, cw.at[0, kept], ref, lane_of(ref, end)))
            if b < LIVE:
                sem = lane_of(w_all.at[b, :, pl.ds(0, 2 * span)], end)
                pieces = []
                for r in range(way, NX, 2):
                    for k in range(SUB):
                        size = span // SUB
                        at = pl.ds(pl.multiple_of(xs[r] * span + k * size, size), size)
                        pieces.append(Piece(b, way, pw.at[0, :, at], w_all.at[b, :, at], sem))
                columns_of.append(pieces)

    def launch(b, pieces):
        @pl.when(z == b)
        def _():
            for piece in pieces:
                piece.first.start()
            for piece in pieces:
                pltpu.make_async_copy(piece.src, piece.ref, piece.sem).start()

    def both(b):
        return [piece for two in zip(columns_of[2 * b], columns_of[2 * b + 1]) for piece in two]

    def relays(pieces, hop, lo=0, hi=None):
        for piece in pieces[lo:hi]:
            piece.relay(hop)

    head_core = link(heads.at[x, y, c], heads.at[x, y, c], sibling, last)
    head_x = [link(heads.at[x, y], heads.at[x, y], at_x[r], last) for r in range(NX - 1)]
    head_y = [link(heads.at[:, y], heads.at[:, y], at_y[r], last) for r in range(NY - 1)]
    w3h_out = [link(w3h, w3h, {"section": zs[r]}, last) for r in range(NZ - 1)]

    launch(0, taps_of[:2] + both(0))
    for b in range(1, NZ):
        launch(b, taps_of[2 * b : 2 * b + 2])
    launch(1, columns_of[3])

    wait_bytes(labels_in, local_sem.at[2])
    wait_bytes(head_in, local_sem.at[3])
    picked = (
        lax.broadcasted_iota(jnp.int32, (head.shape[0], CLASSES), 0)
        == lax.broadcasted_iota(jnp.int32, (head.shape[0], CLASSES), 1)
    ).astype(F32)
    head[...] = nt(picked, head_raw[...].astype(F32))

    @pl.when(last)
    def _():
        heads[x, y, c] = head[...]
        head_core.start()

    for piece in taps_of[:2] + both(0)[: 2 * SUB]:
        piece.relay(0)
        piece.relay(1)

    @pl.when(last)
    def _():
        head_core.wait_recv()
        for copy in head_x:
            copy.start()

    lane = lax.broadcasted_iota(jnp.int32, (group, width), 1)
    first_group = lane < group
    edge = 8
    pad[pl.ds(0, edge), :] = jnp.zeros((edge, width), F32)
    pad[pl.ds(edge + steps, edge), :] = jnp.zeros((edge, width), F32)
    wait_bytes(start, local_sem.at[0])
    state[...] = start[...].astype(F32)

    def unfold(b):
        pad[pl.ds(edge, steps), :] = state[...]
        for k in range(taps):
            cols[b, :, pl.ds(k * width, width)] = pad[pl.ds(edge + k - half, steps), :].astype(BF16)

    def widen(b):
        for piece in taps_of[2 * b : 2 * b + 2]:
            piece.ready()
        for k in range(taps):
            tap = cw_all[b, k].astype(F32)
            dense[b, pl.ds(k * width, group), :] = jnp.where(first_group, tap, 0.0).astype(BF16)
            dense[b, pl.ds(k * width + group, group), :] = jnp.where(first_group, 0.0, tap).astype(BF16)

    def conv(b):
        value = nn(cols[b], dense[b])
        conv_out[b] = value
        act[b] = (value * jax.nn.sigmoid(value)).astype(BF16)

    unfold(0)
    for piece in both(0)[2 * SUB : 3 * SUB]:
        piece.relay(0)
        piece.relay(1)

    @pl.when(last)
    def _():
        for copy in head_x:
            copy.wait_recv()
        for copy in head_y:
            copy.start()

    widen(0)
    conv(0)
    for piece in both(0)[3 * SUB :]:
        piece.relay(0)
        piece.relay(1)
    relays(taps_of[2:], 0)
    launch(1, columns_of[2])
    launch(2, columns_of[5])

    def mix(b):
        ca = fan([(pas.at[b, r], par.at[b, r], sibling) for r in range(NX)], pas.at[b])
        cb = fan([(pbs.at[b, r], pbr.at[b, r], sibling) for r in range(NY)], pbs.at[b])
        a1 = fan([(sa.at[b, r], r1a.at[b, r], at_x[r]) for r in range(NX - 1)], r1a.at[b])
        b1 = fan([(sb.at[b, r], r1b.at[b, r], at_y[r]) for r in range(NY - 1)], r1b.at[b])
        a2 = fan([(s1a.at[b, r], r2a.at[b, r], at_y[r]) for r in range(NY - 1)], r2a.at[b])
        b2 = fan([(s1b.at[b, r], r2b.at[b, r], at_x[r]) for r in range(NX - 1)], r2b.at[b])

        def weights(place, core):
            return jnp.concatenate(
                [
                    w_all[b, :, pl.ds(pl.multiple_of(place(j) * pair + core * width, width), width)]
                    for j in range(NY)
                ],
                axis=1,
            )

        def line_a(r):
            return lambda j: xs[r] * NY + j

        def line_b(r):
            return lambda i: i * NY + ys[r]

        for piece in both(b):
            piece.ready()
        for r in range(NX + 1):
            if r < NX:
                for rows, line, out, copy in ((rows_a, line_a, pas, ca), (rows_b, line_b, pbs, cb)):
                    part = nn(act[b, rows, :], weights(line(r), other))
                    for j in range(NY):
                        out[b, r, j] = part[:, j * width : (j + 1) * width].astype(BF16)
                    copy[r].start()
            if r >= 1:
                q = r - 1
                for rows, line, heard, out, copy, first in (
                    (rows_a, line_a, par, sa, ca, a1),
                    (rows_b, line_b, pbr, sb, cb, b1),
                ):
                    part = nn(act[b, rows, :], weights(line(q), c))
                    copy[q].wait_recv()
                    for j in range(NY):
                        out[b, q, j] = (
                            part[:, j * width : (j + 1) * width] + heard[b, q, j].astype(F32)
                        ).astype(BF16)
                    if q < NX - 1:
                        first[q].start()
        if b == 0:
            relays(taps_of[2:], 1)
            relays(columns_of[2], 0, 0, 5)
            relays(columns_of[3], 1, 0, 5)
        if b == 1:
            relays(columns_of[5], 1, 0, 4)
            relays(columns_of[4], 0, 0, 5)
        kept = []
        for first, second, own, heard, out, seen, mine in (
            (a1, a2, sa, r1a, s1a, ys, y),
            (b1, b2, sb, r1b, s1b, xs, x),
        ):
            for copy in first:
                copy.wait_recv()
            if first is b1:
                if b == 0:
                    relays(columns_of[2], 0, 5)
                    relays(columns_of[3], 1, 5)
                if b == 1:
                    relays(columns_of[4], 0, 5)

            def total_at(j):
                total = own[b, NX - 1, j].astype(F32)
                for q in range(NX - 1):
                    total = total + heard[b, q, j].astype(F32)
                return total

            for r in range(NX - 1):
                out[b, r] = total_at(seen[r]).astype(BF16)
                second[r].start()
            kept.append(total_at(mine))
        if b == 0:
            launch(2, columns_of[4])
            relays(columns_of[3], 0)
            relays(columns_of[5], 0)
            relays(columns_of[2], 1)
        if b == 1:
            relays(columns_of[5], 1, 4)
            relays(columns_of[4], 1)
        widen(b + 1)
        for rows, second, heard, total in ((rows_a, a2, r2a, kept[0]), (rows_b, b2, r2b, kept[1])):
            for r in range(NX - 1):
                second[r].wait_recv()
                total = total + heard[b, r].astype(F32)
            state[rows, :] = (state[rows, :] + total).astype(BF16).astype(F32)

    for b in range(LIVE):
        if b > 0:
            unfold(b)
            conv(b)
        mix(b)
        if b == 0:
            @pl.when(last)
            def _():
                for copy in head_y:
                    copy.wait_recv()
                wait_bytes(w_last, local_sem.at[1])

                def fold(i, total):
                    whole = jnp.concatenate(
                        [heads[i, j, k] for j in range(NY) for k in range(NC)], axis=1
                    ).astype(BF16)
                    return total + nt(whole, w_last[:, pl.ds(pl.multiple_of(i * span, span), span)])

                w3h[...] = lax.fori_loop(0, NX, fold, jnp.zeros(w3h.shape, F32))
                for copy in w3h_out:
                    copy.start()

    unfold(LIVE)
    conv(LIVE)

    s_core = link(score_own.at[0], score_in.at[0], sibling)
    s_x = [link(score_own.at[1], score_in.at[1 + r], at_x[r]) for r in range(NX - 1)]
    s_y = [link(score_own.at[2], score_in.at[NX + r], at_y[r]) for r in range(NY - 1)]
    for r in range(NZ - 1):
        @pl.when(z == r)
        def _():
            w3h_out[r].wait_recv()

    scores = nt(head[...], state[...], HIGH) + nt(w3h[...], act[LIVE].astype(F32), HIGH)
    score_own[0] = scores
    s_core.start()
    s_core.wait_recv()
    scores = scores + score_in[0]
    score_own[1] = scores
    for copy in s_x:
        copy.start()
    for copy in s_x:
        copy.wait_recv()
    for r in range(NX - 1):
        scores = scores + score_in[1 + r]
    score_own[2] = scores
    for copy in s_y:
        copy.start()
    for copy in s_y:
        copy.wait_recv()
    for r in range(NY - 1):
        scores = scores + score_in[NX + r]
    classes = lax.broadcasted_iota(jnp.int32, scores.shape, 0)
    hot = (classes == labels[pl.ds(z, 1), :]).astype(F32)
    top = (jax.nn.sigmoid(scores) - hot) * (LOSS_SCALE / (NZ * steps))
    top_t = top.T
    back = nn(top_t, head[...], HIGH).astype(BF16).astype(F32)
    act_grad = nn(top_t, w3h[...], HIGH)

    def silu_grad(b, act_grad):
        value = conv_out[b]
        s = jax.nn.sigmoid(value)
        cgrad[b] = (act_grad * s * (1.0 + value * (1.0 - s))).astype(BF16)

    def input_grad(b):
        pad[pl.ds(edge, steps), :] = cgrad[b].astype(F32)
        total = jnp.zeros((steps, width), F32)
        for k in range(taps):
            shifted = pad[pl.ds(edge - k + half, steps), :].astype(BF16)
            total = total + nt(shifted, dense[b, pl.ds(k * width, width), :])
        return total

    starts = [1, 3]
    middles = [(2, 3), (2, 1)]
    home_sems = [recv.at[number()] for _ in range(NZ - 1)]

    def conv_weight_grad(b):
        whole = tn(cols[b], cgrad[b])
        sem = lane_of(gcsend.at[b], z != b)

        def piece(k):
            return jnp.where(
                first_group,
                whole[k * width : k * width + group],
                whole[k * width + group : (k + 1) * width],
            )

        @pl.when(z == b)
        def _():
            for k in range(taps):
                gcpart[k] = piece(k)

        @pl.when(z != b)
        def _():
            for k in range(taps):
                gcsend[b, k] = piece(k).astype(BF16)

        for d in range(1, NZ):
            @pl.when(is_z(b + d))
            def _():
                remote(
                    gcsend.at[b], gccrecv.at[d - 1], sem, home_sems[d - 1], {"section": jnp.int32(b)}
                ).start()

    def gather_links(b):
        own_a, own_b = ga.at[b, NX - 1, NY - 1, c], gb.at[b, NY - 1, NX - 1, c]
        three = r2a.at[0]
        rest = pl.ds(0, NX - 1)
        nine = r1a.at[0, rest, rest]
        line_a, line_b = ga.at[b, NX - 1, rest, c], gb.at[b, NY - 1, rest, c]
        links = {
            "a1": fan([(own_a, ga.at[b, NX - 1, r, c], at_y[r]) for r in range(NY - 1)], three),
            "b1": fan([(own_b, gb.at[b, NY - 1, r, c], at_x[r]) for r in range(NX - 1)], three),
            "a2own": fan([(own_a, ga.at[b, r, NY - 1, c], at_x[r]) for r in range(NX - 1)], three),
            "b2own": fan([(own_b, gb.at[b, r, NX - 1, c], at_y[r]) for r in range(NY - 1)], three),
            "a2": fan([(line_a, ga.at[b, r, rest, c], at_x[r]) for r in range(NX - 1)], nine),
            "b2": fan([(line_b, gb.at[b, r, rest, c], at_y[r]) for r in range(NY - 1)], nine),
            "ca": fan([(ga.at[b, r, :, c], ga.at[b, r, :, c], sibling) for r in range(NX)], pas.at[0]),
            "cb": fan([(gb.at[b, r, :, c], gb.at[b, r, :, c], sibling) for r in range(NY)], pbs.at[0]),
        }
        return links

    def gather_start(b, links, back):
        ga[b, NX - 1, NY - 1, c] = back[:top_rows].astype(BF16)
        gb[b, NY - 1, NX - 1, c] = back[top_rows:].astype(BF16)
        for name in ("a1", "b1", "a2own", "b2own"):
            for copy in links[name]:
                copy.start()

    def gather_second(links):
        for p in "ab":
            for copy in links[p + "1"]:
                copy.wait_recv()
            for copy in links[p + "2"]:
                copy.start()
            links["c" + p][NX - 1].start()

    def gather_third(links):
        for r in range(NX - 1):
            for p in "ab":
                links[p + "2own"][r].wait_recv()
                links[p + "2"][r].wait_recv()
                links["c" + p][r].start()

    def pair_cols(px, py):
        return pl.ds(pl.multiple_of((px * NY + py) * pair, pair), pair)

    def act_grad_of(b, links):
        totals = [jnp.zeros((top_rows, width), F32) for _ in range(2)]
        for r in [NX - 1] + list(range(NX - 1)):
            for way, buffer in enumerate((ga, gb)):
                links[("ca", "cb")[way]][r].wait_recv()
                left = jnp.concatenate([buffer[b, r, s, k] for s in range(NY) for k in range(NC)], axis=1)
                right = jnp.concatenate(
                    [
                        w_all[b, :, pair_cols(xl[r], yl[s]) if way == 0 else pair_cols(xl[s], yl[r])]
                        for s in range(NY)
                    ],
                    axis=1,
                )
                totals[way] = totals[way] + nt(left, right)
        return jnp.concatenate(totals, axis=0)

    def home_copy(b, side, r, s):
        return remote(
            gsend.at[b, r, s], hrecv.at[side, r, s], gp_send.at[b], home_gp.at[side, r, s], (down, up)[side]
        )

    def gp_copy(b, r, s, device):
        return remote(gsend.at[b, r, s], crecv.at[b, r, s], gp_send.at[b], gp_recv.at[b, r, s], device)

    def point_grad(b):
        act_t = act[b].astype(F32).T.astype(BF16)
        turn = jnp.where(is_z(b + starts[0]), 2, 0)
        starter = is_z(b + starts[0], b + starts[1])
        device = {"section": jnp.where(is_z(b + starts[0]), zs[0], zs[2])}
        for slot in range(NX):
            r = lax.rem(slot + turn, NX)
            for s in range(NY):
                whole = jnp.concatenate(
                    [
                        jnp.concatenate([ga[b, r, s, k] for k in range(NC)], axis=1),
                        jnp.concatenate([gb[b, s, r, k] for k in range(NC)], axis=1),
                    ],
                    axis=0,
                )
                part = nn(act_t, whole)
                if slot < 2 and b == 0:
                    @pl.when(starter)
                    def _():
                        gsend[b, r, s] = part.astype(BF16)
                        gp_copy(b, r, s, device).start()

                    @pl.when(jnp.logical_not(starter))
                    def _():
                        gpart[b % 2, r, s] = part
                elif b > 0:
                    far = is_z(b + 2)

                    @pl.when(far)
                    def _():
                        gsend[b, r, s] = part.astype(BF16)
                        gp_copy(b, r, s, (down, up)[slot // 2]).start()

                    if slot < 2:
                        for side in range(2):
                            @pl.when(is_z(b + starts[side]))
                            def _():
                                gsend[b, r, s] = part.astype(BF16)
                                home_copy(b, side, r, s).start()

                        @pl.when(z == b)
                        def _():
                            gpart[b % 2, r, s] = part
                    else:
                        @pl.when(jnp.logical_not(far))
                        def _():
                            gpart[b % 2, r, s] = part
                else:
                    gpart[b % 2, r, s] = part

        @pl.when(z == b)
        def _():
            ghome[...] = gpart[b % 2]

    def side_relay(b, lo, hi):
        for j in range(lo, hi):
            for side in range(2):
                r, s = 2 * side + j // NY, j % NY

                @pl.when(is_z(b + starts[side]))
                def _():
                    gp_copy(b, r, s, up).wait_recv()
                    gsend[b, r, s] = (gpart[b % 2, r, s] + crecv[b, r, s].astype(F32)).astype(BF16)
                    home_copy(b, side, r, s).start()

    def point_relay(b, hop, lo, hi):
        for j in range(lo, hi):
            for way in range(2):
                r, s = (2 if way == 0 else 0) + j // NY, j % NY

                @pl.when(is_z(b + middles[way][hop]))
                def _():
                    copy = gp_copy(b, r, s, (up, down)[way])
                    copy.wait_recv()
                    gsend[b, r, s] = (gpart[b % 2, r, s] + crecv[b, r, s].astype(F32)).astype(BF16)
                    copy.start()

    silu_grad(LIVE, act_grad)
    back = (back + input_grad(LIVE)).astype(BF16).astype(F32)
    links = gather_links(LIVE - 1)
    gather_start(LIVE - 1, links, back)
    tsend[...] = nn(top, act[LIVE].astype(F32), HIGH)
    t_sem = lane_of(tsend, z != NZ - 1)
    t_links = [
        remote(tsend, trecv.at[d - 1], t_sem, recv.at[number()], {"section": jnp.int32(NZ - 1)})
        for d in range(1, NZ)
    ]
    for d in range(1, NZ):
        @pl.when(z == (NZ - 1 + d) % NZ)
        def _():
            t_links[d - 1].start()

    gather_second(links)
    conv_weight_grad(LIVE)
    for b in range(LIVE - 1, -1, -1):
        if b + 2 < LIVE:
            side_relay(b + 2, 0, 8)
        gather_third(links)
        silu_grad(b, act_grad_of(b, links))
        if b > 0:
            back = (back + input_grad(b)).astype(BF16).astype(F32)
            links = gather_links(b - 1)
            gather_start(b - 1, links, back)
        point_grad(b)
        if b > 0:
            gather_second(links)
        conv_weight_grad(b)
    side_relay(1, 0, 8)
    for j in range(0, 8, 2):
        point_relay(0, 0, j, j + 2)
        if j:
            point_relay(0, 1, j - 2, j)
    point_relay(0, 1, 6, 8)

    def out_copy(r, s):
        return pltpu.make_async_copy(
            ghome.at[r, s], out_gp.at[0, :, pair_cols(xl[r], yl[s])], out_sem.at[0]
        )

    @pl.when(last)
    def _():
        total = tsend[...]
        for d in range(1, NZ):
            t_links[d - 1].wait_recv()
            total = total + trecv[d - 1]
        total_t = total.T
        for r in range(NX):
            for s in range(NY):
                whole = jnp.concatenate([heads[xl[r], yl[s], k] for k in range(NC)], axis=1)
                ghome[r, s] = nn(total_t, whole, HIGH)
                out_copy(r, s).start()

    for b in range(LIVE):
        @pl.when(z == b)
        def _():
            for j in range(2 * NY):
                for r, s in ((2 + j // NY, j % NY), (j // NY, j % NY)):
                    if b == 0:
                        gp_copy(b, r, s, up).wait_recv()
                        heard = crecv[b, r, s].astype(F32)
                    else:
                        for side in range(2):
                            home_copy(b, side, r, s).wait_recv()
                        heard = hrecv[0, r, s].astype(F32) + hrecv[1, r, s].astype(F32)
                    ghome[r, s] = ghome[r, s] + heard
                    out_copy(r, s).start()

    total = gcpart[...]
    for d in range(1, NZ):
        wait_bytes(gccrecv.at[d - 1], home_sems[d - 1])
        total = total + gccrecv[d - 1].astype(F32)
    gcpart[...] = total
    gc_out = pltpu.make_async_copy(gcpart, out_gc.at[0], out_sem.at[1])
    gc_out.start()
    for b in range(LIVE):
        drains.append((gsend.at[b], gp_send.at[b], z != b))
    for ref, sem, when in drains:
        if when is None:
            wait_bytes(ref, sem)
        else:
            pl.when(when)(functools.partial(wait_bytes, ref, sem))
    wait_bytes(ghome, out_sem.at[0])
    gc_out.wait()
    assert sends[0] <= send.shape[0], sends[0]
    assert count[0] <= recv.shape[0], count[0]


def local(inputs, labels, conv_weight, point_weight, head_weight):
    steps, width = inputs.shape[1:]
    blocks, taps, group, _ = conv_weight.shape
    chans = point_weight.shape[2]
    part = steps // 2
    pair = NC * width
    hbm = pl.BlockSpec(memory_space=pl.ANY)
    V = pltpu.VMEM
    dma = pltpu.SemaphoreType.DMA
    scratch = [
        V(labels.shape, labels.dtype),
        V(head_weight.shape, BF16),
        V((8, width), F32),
        V((LIVE, width, chans), BF16),
        V((NZ, taps, group, width), BF16),
        V((width, chans), BF16),
        V((steps, width), BF16),
        V((NZ, taps * width, width), BF16),
        V((NZ, steps, taps * width), BF16),
        V((NZ, steps, width), F32),
        V((NZ, steps, width), BF16),
        V((steps, width), F32),
        V((steps + 16, width), F32),
        V((NZ, steps, width), BF16),
        V((LIVE, NX, NY, part, width), BF16),
        V((LIVE, NX, NY, part, width), BF16),
        V((LIVE, NY, NX, part, width), BF16),
        V((LIVE, NY, NX, part, width), BF16),
        V((LIVE, NX, NY, part, width), BF16),
        V((LIVE, NY, NX, part, width), BF16),
        V((LIVE, NX - 1, NY, part, width), BF16),
        V((LIVE, NY - 1, NX, part, width), BF16),
        V((LIVE, NY - 1, part, width), BF16),
        V((LIVE, NX - 1, part, width), BF16),
        V((LIVE, NY - 1, part, width), BF16),
        V((LIVE, NX - 1, part, width), BF16),
        V((LIVE, NX, NY, NC, part, width), BF16),
        V((LIVE, NY, NX, NC, part, width), BF16),
        V((LIVE, NX, NY, width, pair), BF16),
        V((LIVE, NX, NY, width, pair), BF16),
        V((2, NX, NY, width, pair), BF16),
        V((2, NX, NY, width, pair), F32),
        V((NX, NY, width, pair), F32),
        V((NZ, taps, group, width), BF16),
        V((NZ - 1, taps, group, width), BF16),
        V((taps, group, width), F32),
        V((NX, NY, NC, 8, width), F32),
        V((8, width), F32),
        V((8, width), F32),
        V((NZ - 1, 8, width), F32),
        V((3, 8, steps), F32),
        V((NX + NY - 1, 8, steps), F32),
        dma((80,)),
        dma((222,)),
        dma((LIVE,)),
        dma((LIVE, NX, NY)),
        dma((2, NX, NY)),
        dma((4,)),
        dma((2,)),
    ]
    return pl.pallas_call(
        kernel,
        out_shape=(
            jax.ShapeDtypeStruct(point_weight.shape, F32),
            jax.ShapeDtypeStruct(conv_weight.shape, F32),
        ),
        in_specs=[hbm] * 5,
        out_specs=(hbm, hbm),
        scratch_shapes=scratch,
        compiler_params=pltpu.CompilerParams(
            collective_id=0, has_side_effects=True, vmem_limit_bytes=58 * 1024 * 1024
        ),
    )(inputs, labels, conv_weight, point_weight, head_weight)


def solution(mesh):
    placed = (
        P(None, None, "chan"),
        P(),
        P("section", None, None, "chan"),
        P("section", "chan", None),
        P("chan", None),
    )
    return jax.shard_map(
        local,
        mesh=mesh,
        in_specs=placed,
        out_specs=(P("section", "chan", None), P("section", None, None, "chan")),
        check_vma=False,
    )
```

```python
import functools

import jax
import jax.numpy as jnp
from jax import lax
from jax.experimental import pallas as pl
from jax.experimental.pallas import tpu as pltpu
from jax.sharding import PartitionSpec as P

CLASSES = 3
LOSS_SCALE = 2048
NX, NY, NC, NZ = 4, 4, 2, 4
LIVE = 3
SUB = 4
F32, BF16 = jnp.float32, jnp.bfloat16
HIGH = lax.Precision.HIGHEST
MESH = pl.DeviceIdType.MESH


def nn(a, b, precision=None):
    return lax.dot_general(a, b, (((1,), (0,)), ((), ())), precision=precision, preferred_element_type=F32)


def nt(a, b, precision=None):
    return lax.dot_general(a, b, (((1,), (1,)), ((), ())), precision=precision, preferred_element_type=F32)


def tn(a, b, precision=None):
    return lax.dot_general(a, b, (((0,), (0,)), ((), ())), precision=precision, preferred_element_type=F32)


def wait_bytes(ref, sem):
    pltpu.make_async_copy(ref, ref, sem).wait()


def kernel(
    inputs, labels_in, cw, pw, head_in,
    out_gp, out_gc,
    labels, head_raw, head, w_all, cw_all, w_last, start, dense, cols, conv_out, act, state, pad, cgrad,
    pas, par, pbs, pbr, sa, sb, r1a, r1b, s1a, s1b, r2a, r2b,
    ga, gb, gsend, crecv, hrecv, gpart, ghome, gcsend, gccrecv, gcpart,
    heads, w3h, tsend, trecv, score_own, score_in,
    send, recv, gp_send, gp_recv, home_gp, local_sem, out_sem,
):
    steps, width = start.shape
    taps, group = cw.shape[1], cw.shape[2]
    half = taps // 2
    top_rows = steps // 2
    pair = NC * width
    span = NY * pair
    rows_a, rows_b = pl.ds(0, top_rows), pl.ds(top_rows, top_rows)
    z = lax.axis_index("section")
    me = lax.axis_index("chan")
    c = lax.rem(me, NC)
    y = lax.rem(lax.div(me, NC), NY)
    x = lax.div(me, NC * NY)
    other = 1 - c
    sibling = {"chan": me + 1 - 2 * c}
    xs = [lax.rem(x + 1 + r, NX) for r in range(NX)]
    ys = [lax.rem(y + 1 + r, NY) for r in range(NY)]
    xl = [lax.rem(x + NX - 1 - r, NX) for r in range(NX)]
    yl = [lax.rem(y + NY - 1 - r, NY) for r in range(NY)]
    at_x = [{"chan": (xs[r] * NY + y) * NC + c} for r in range(NX - 1)]
    at_y = [{"chan": (x * NY + ys[r]) * NC + c} for r in range(NY - 1)]
    zs = [lax.rem(z + 1 + r, NZ) for r in range(NZ - 1)]
    up, down = {"section": zs[0]}, {"section": zs[2]}
    last = z == NZ - 1

    def is_z(*places):
        hit = z == places[0] % NZ
        for place in places[1:]:
            hit = hit | (z == place % NZ)
        return hit

    count = [0]

    def number():
        count[0] += 1
        return count[0] - 1

    def remote(src, dst, send_sem, recv_sem, device):
        return pltpu.make_async_remote_copy(
            src_ref=src, dst_ref=dst, send_sem=send_sem, recv_sem=recv_sem,
            device_id=device, device_id_type=MESH,
        )

    sends = [0]
    drains = []

    def lane_of(total, when=None):
        sends[0] += 1
        sem = send.at[sends[0] - 1]
        drains.append((total, sem, when))
        return sem

    def fan(copies, total, when=None):
        sem = lane_of(total, when)
        return [remote(src, dst, sem, recv.at[number()], device) for src, dst, device in copies]

    def link(src, dst, device, when=None):
        return fan([(src, dst, device)], src, when)[0]

    pltpu.make_async_copy(inputs.at[z], start, local_sem.at[0]).start()
    pltpu.make_async_copy(labels_in, labels, local_sem.at[2]).start()
    pltpu.make_async_copy(head_in, head_raw, local_sem.at[3]).start()

    @pl.when(last)
    def _():
        pltpu.make_async_copy(pw.at[0], w_last, local_sem.at[1]).start()

    barrier = pltpu.get_barrier_semaphore()
    peers = [sibling] + at_x + at_y + [{"section": s} for s in zs]
    for peer in peers:
        pl.semaphore_signal(barrier, inc=1, device_id=peer, device_id_type=MESH)
    pl.semaphore_wait(barrier, len(peers))

    class Piece:
        def __init__(self, b, way, src, ref, sem):
            self.src, self.ref, self.sem = src, ref, recv.at[number()]
            device = (up, down)[way]
            self.order = [b + 1, b + 2, b + 3] if way == 0 else [b + 3, b + 2, b + 1]
            self.first = remote(src, ref, sem, self.sem, device)
            self.next = remote(ref, ref, sem, self.sem, device)

        def relay(self, hop):
            @pl.when(is_z(self.order[hop]))
            def _():
                wait_bytes(self.ref, self.sem)
                self.next.start()

        def ready(self):
            @pl.when(jnp.logical_not(is_z(*self.order[:2])))
            def _():
                wait_bytes(self.ref, self.sem)

    taps_of, columns_of = [], []
    for b in range(NZ):
        for way in range(2):
            end = z != (b + (3, 1)[way]) % NZ
            kept = pl.ds(0, half + 1) if way == 0 else pl.ds(half + 1, taps - half - 1)
            ref = cw_all.at[b, kept]
            taps_of.append(Piece(b, way, cw.at[0, kept], ref, lane_of(ref, end)))
            if b < LIVE:
                sem = lane_of(w_all.at[b, :, pl.ds(0, 2 * span)], end)
                pieces = []
                for r in range(way, NX, 2):
                    for k in range(SUB):
                        size = span // SUB
                        at = pl.ds(pl.multiple_of(xs[r] * span + k * size, size), size)
                        pieces.append(Piece(b, way, pw.at[0, :, at], w_all.at[b, :, at], sem))
                columns_of.append(pieces)

    def launch(b, pieces):
        @pl.when(z == b)
        def _():
            for piece in pieces:
                piece.first.start()
            for piece in pieces:
                pltpu.make_async_copy(piece.src, piece.ref, piece.sem).start()

    def both(b):
        return [piece for two in zip(columns_of[2 * b], columns_of[2 * b + 1]) for piece in two]

    def relays(pieces, hop, lo=0, hi=None):
        for piece in pieces[lo:hi]:
            piece.relay(hop)

    head_core = link(heads.at[x, y, c], heads.at[x, y, c], sibling, last)
    head_x = [link(heads.at[x, y], heads.at[x, y], at_x[r], last) for r in range(NX - 1)]
    head_y = [link(heads.at[:, y], heads.at[:, y], at_y[r], last) for r in range(NY - 1)]
    w3h_out = [link(w3h, w3h, {"section": zs[r]}, last) for r in range(NZ - 1)]

    launch(0, taps_of[:2] + both(0))
    for b in range(1, NZ):
        launch(b, taps_of[2 * b : 2 * b + 2])
    launch(1, columns_of[3])

    wait_bytes(labels_in, local_sem.at[2])
    wait_bytes(head_in, local_sem.at[3])
    picked = (
        lax.broadcasted_iota(jnp.int32, (head.shape[0], CLASSES), 0)
        == lax.broadcasted_iota(jnp.int32, (head.shape[0], CLASSES), 1)
    ).astype(F32)
    head[...] = nt(picked, head_raw[...].astype(F32))

    @pl.when(last)
    def _():
        heads[x, y, c] = head[...]
        head_core.start()

    for piece in taps_of[:2] + both(0)[: 2 * SUB]:
        piece.relay(0)
        piece.relay(1)

    @pl.when(last)
    def _():
        head_core.wait_recv()
        for copy in head_x:
            copy.start()

    lane = lax.broadcasted_iota(jnp.int32, (group, width), 1)
    first_group = lane < group
    edge = 8
    pad[pl.ds(0, edge), :] = jnp.zeros((edge, width), F32)
    pad[pl.ds(edge + steps, edge), :] = jnp.zeros((edge, width), F32)
    wait_bytes(start, local_sem.at[0])
    state[...] = start[...].astype(F32)

    def unfold(b):
        pad[pl.ds(edge, steps), :] = state[...]
        for k in range(taps):
            cols[b, :, pl.ds(k * width, width)] = pad[pl.ds(edge + k - half, steps), :].astype(BF16)

    def widen(b):
        for piece in taps_of[2 * b : 2 * b + 2]:
            piece.ready()
        for k in range(taps):
            tap = cw_all[b, k].astype(F32)
            dense[b, pl.ds(k * width, group), :] = jnp.where(first_group, tap, 0.0).astype(BF16)
            dense[b, pl.ds(k * width + group, group), :] = jnp.where(first_group, 0.0, tap).astype(BF16)

    def conv(b):
        value = nn(cols[b], dense[b])
        conv_out[b] = value
        act[b] = (value * jax.nn.sigmoid(value)).astype(BF16)

    unfold(0)
    relays(taps_of[2:], 0)
    for piece in both(0)[2 * SUB : 3 * SUB]:
        piece.relay(0)
        piece.relay(1)

    @pl.when(last)
    def _():
        for copy in head_x:
            copy.wait_recv()
        for copy in head_y:
            copy.start()

    widen(0)
    conv(0)
    for piece in both(0)[3 * SUB :]:
        piece.relay(0)
        piece.relay(1)
    relays(taps_of[2:], 1)

    @pl.when(z == 0)
    def _():
        for piece in columns_of[3]:
            wait_bytes(piece.ref, piece.sem)
        for piece in columns_of[3]:
            piece.next.start()

    launch(1, columns_of[2])
    launch(2, columns_of[5])

    up1, down1, up2, down2 = columns_of[2:6]
    plan = {
        (0, "early"): [(down1, 1, 0, 4), (up1, 0, 0, 1)],
        (0, 1): [(down1, 1, 4, 5), (up1, 0, 1, 2)],
        (0, 2): [(down1, 1, 5, 6), (up1, 0, 2, 3)],
        (0, 3): [(up1, 0, 3, 4)],
        (0, 4): [(down1, 1, 6, 7)],
        (0, "sent"): [(down1, 1, 7, 8), (up1, 0, 4, 6), (up1, 1, 0, 2), (down2, 0, 0, 2)],
        (0, "middle"): [(up1, 0, 6, 8), (up1, 1, 2, 5), (down2, 0, 2, 5)],
        (0, "late"): [(up1, 1, 5, 8), (down2, 0, 5, 8)],
        (1, "early"): [(down2, 1, 0, 5)],
        (1, 1): [(down2, 1, 5, 6), (up2, 0, 0, 1)],
        (1, 2): [(down2, 1, 6, 7), (up2, 0, 1, 2)],
        (1, 3): [(down2, 1, 7, 8), (up2, 0, 2, 3)],
        (1, "sent"): [(up2, 0, 3, 4), (up2, 1, 0, 1)],
        (1, "middle"): [(up2, 0, 4, 7), (up2, 1, 1, 4)],
        (1, "late"): [(up2, 0, 7, 8), (up2, 1, 4, 7)],
        (1, "after"): [(up2, 1, 7, 8)],
    }

    def slot(b, name):
        for pieces, hop, lo, hi in plan.get((b, name), []):
            relays(pieces, hop, lo, hi)
        if (b, name) == (0, "middle"):
            launch(2, up2)

    def mix(b):
        ca = fan([(pas.at[b, r], par.at[b, r], sibling) for r in range(NX)], pas.at[b])
        cb = fan([(pbs.at[b, r], pbr.at[b, r], sibling) for r in range(NY)], pbs.at[b])
        a1 = fan([(sa.at[b, r], r1a.at[b, r], at_x[r]) for r in range(NX - 1)], r1a.at[b])
        b1 = fan([(sb.at[b, r], r1b.at[b, r], at_y[r]) for r in range(NY - 1)], r1b.at[b])
        a2 = fan([(s1a.at[b, r], r2a.at[b, r], at_y[r]) for r in range(NY - 1)], r2a.at[b])
        b2 = fan([(s1b.at[b, r], r2b.at[b, r], at_x[r]) for r in range(NX - 1)], r2b.at[b])

        def weights(place, core):
            return jnp.concatenate(
                [
                    w_all[b, :, pl.ds(pl.multiple_of(place(j) * pair + core * width, width), width)]
                    for j in range(NY)
                ],
                axis=1,
            )

        def line_a(r):
            return lambda j: xs[r] * NY + j

        def line_b(r):
            return lambda i: i * NY + ys[r]

        slot(b, "early")
        for piece in both(b):
            piece.ready()
        for r in range(NX + 1):
            if r < NX:
                for rows, line, out, copy in ((rows_a, line_a, pas, ca), (rows_b, line_b, pbs, cb)):
                    part = nn(act[b, rows, :], weights(line(r), other))
                    for j in range(NY):
                        out[b, r, j] = part[:, j * width : (j + 1) * width].astype(BF16)
                    copy[r].start()
            slot(b, r)
            if r >= 1:
                q = r - 1
                for rows, line, heard, out, copy, first in (
                    (rows_a, line_a, par, sa, ca, a1),
                    (rows_b, line_b, pbr, sb, cb, b1),
                ):
                    part = nn(act[b, rows, :], weights(line(q), c))
                    copy[q].wait_recv()
                    for j in range(NY):
                        out[b, q, j] = (
                            part[:, j * width : (j + 1) * width] + heard[b, q, j].astype(F32)
                        ).astype(BF16)
                    if q < NX - 1:
                        first[q].start()
        slot(b, "sent")
        kept = []
        for first, second, own, heard, out, seen, mine in (
            (a1, a2, sa, r1a, s1a, ys, y),
            (b1, b2, sb, r1b, s1b, xs, x),
        ):
            for copy in first:
                copy.wait_recv()
            if first is b1:
                slot(b, "middle")

            def total_at(j):
                total = own[b, NX - 1, j].astype(F32)
                for q in range(NX - 1):
                    total = total + heard[b, q, j].astype(F32)
                return total

            for r in range(NX - 1):
                out[b, r] = total_at(seen[r]).astype(BF16)
                second[r].start()
            kept.append(total_at(mine))
        slot(b, "late")
        widen(b + 1)
        for rows, second, heard, total in ((rows_a, a2, r2a, kept[0]), (rows_b, b2, r2b, kept[1])):
            for r in range(NX - 1):
                second[r].wait_recv()
                total = total + heard[b, r].astype(F32)
            state[rows, :] = (state[rows, :] + total).astype(BF16).astype(F32)

    for b in range(LIVE):
        if b > 0:
            slot(b - 1, "after")
        if b > 0:
            unfold(b)
            conv(b)
        mix(b)
        if b == 0:
            @pl.when(last)
            def _():
                for copy in head_y:
                    copy.wait_recv()
                wait_bytes(w_last, local_sem.at[1])

                def fold(i, total):
                    whole = jnp.concatenate(
                        [heads[i, j, k] for j in range(NY) for k in range(NC)], axis=1
                    ).astype(BF16)
                    return total + nt(whole, w_last[:, pl.ds(pl.multiple_of(i * span, span), span)])

                w3h[...] = lax.fori_loop(0, NX, fold, jnp.zeros(w3h.shape, F32))
                for copy in w3h_out:
                    copy.start()

    unfold(LIVE)
    conv(LIVE)

    s_core = link(score_own.at[0], score_in.at[0], sibling)
    s_x = [link(score_own.at[1], score_in.at[1 + r], at_x[r]) for r in range(NX - 1)]
    s_y = [link(score_own.at[2], score_in.at[NX + r], at_y[r]) for r in range(NY - 1)]
    for r in range(NZ - 1):
        @pl.when(z == r)
        def _():
            w3h_out[r].wait_recv()

    scores = nt(head[...], state[...], HIGH) + nt(w3h[...], act[LIVE].astype(F32), HIGH)
    score_own[0] = scores
    s_core.start()
    s_core.wait_recv()
    scores = scores + score_in[0]
    score_own[1] = scores
    for copy in s_x:
        copy.start()
    for copy in s_x:
        copy.wait_recv()
    for r in range(NX - 1):
        scores = scores + score_in[1 + r]
    score_own[2] = scores
    for copy in s_y:
        copy.start()
    for copy in s_y:
        copy.wait_recv()
    for r in range(NY - 1):
        scores = scores + score_in[NX + r]
    classes = lax.broadcasted_iota(jnp.int32, scores.shape, 0)
    hot = (classes == labels[pl.ds(z, 1), :]).astype(F32)
    top = (jax.nn.sigmoid(scores) - hot) * (LOSS_SCALE / (NZ * steps))
    top_t = top.T
    back = nn(top_t, head[...], HIGH).astype(BF16).astype(F32)
    act_grad = nn(top_t, w3h[...], HIGH)

    def silu_grad(b, act_grad):
        value = conv_out[b]
        s = jax.nn.sigmoid(value)
        cgrad[b] = (act_grad * s * (1.0 + value * (1.0 - s))).astype(BF16)

    def input_grad(b):
        pad[pl.ds(edge, steps), :] = cgrad[b].astype(F32)
        total = jnp.zeros((steps, width), F32)
        for k in range(taps):
            shifted = pad[pl.ds(edge - k + half, steps), :].astype(BF16)
            total = total + nt(shifted, dense[b, pl.ds(k * width, width), :])
        return total

    starts = [1, 3]
    middles = [(2, 3), (2, 1)]
    home_sems = [recv.at[number()] for _ in range(NZ - 1)]

    def conv_weight_grad(b):
        whole = tn(cols[b], cgrad[b])
        sem = lane_of(gcsend.at[b], z != b)

        def piece(k):
            return jnp.where(
                first_group,
                whole[k * width : k * width + group],
                whole[k * width + group : (k + 1) * width],
            )

        @pl.when(z == b)
        def _():
            for k in range(taps):
                gcpart[k] = piece(k)

        @pl.when(z != b)
        def _():
            for k in range(taps):
                gcsend[b, k] = piece(k).astype(BF16)

        for d in range(1, NZ):
            @pl.when(is_z(b + d))
            def _():
                remote(
                    gcsend.at[b], gccrecv.at[d - 1], sem, home_sems[d - 1], {"section": jnp.int32(b)}
                ).start()

    def gather_links(b):
        own_a, own_b = ga.at[b, NX - 1, NY - 1, c], gb.at[b, NY - 1, NX - 1, c]
        three = r2a.at[0]
        rest = pl.ds(0, NX - 1)
        nine = r1a.at[0, rest, rest]
        line_a, line_b = ga.at[b, NX - 1, rest, c], gb.at[b, NY - 1, rest, c]
        links = {
            "a1": fan([(own_a, ga.at[b, NX - 1, r, c], at_y[r]) for r in range(NY - 1)], three),
            "b1": fan([(own_b, gb.at[b, NY - 1, r, c], at_x[r]) for r in range(NX - 1)], three),
            "a2own": fan([(own_a, ga.at[b, r, NY - 1, c], at_x[r]) for r in range(NX - 1)], three),
            "b2own": fan([(own_b, gb.at[b, r, NX - 1, c], at_y[r]) for r in range(NY - 1)], three),
            "a2": fan([(line_a, ga.at[b, r, rest, c], at_x[r]) for r in range(NX - 1)], nine),
            "b2": fan([(line_b, gb.at[b, r, rest, c], at_y[r]) for r in range(NY - 1)], nine),
            "ca": fan([(ga.at[b, r, :, c], ga.at[b, r, :, c], sibling) for r in range(NX)], pas.at[0]),
            "cb": fan([(gb.at[b, r, :, c], gb.at[b, r, :, c], sibling) for r in range(NY)], pbs.at[0]),
        }
        return links

    def gather_start(b, links, back):
        ga[b, NX - 1, NY - 1, c] = back[:top_rows].astype(BF16)
        gb[b, NY - 1, NX - 1, c] = back[top_rows:].astype(BF16)
        for name in ("a1", "b1", "a2own", "b2own"):
            for copy in links[name]:
                copy.start()

    def gather_second(links):
        for p in "ab":
            for copy in links[p + "1"]:
                copy.wait_recv()
            for copy in links[p + "2"]:
                copy.start()
            links["c" + p][NX - 1].start()

    def gather_third(links):
        for r in range(NX - 1):
            for p in "ab":
                links[p + "2own"][r].wait_recv()
                links[p + "2"][r].wait_recv()
                links["c" + p][r].start()

    def pair_cols(px, py):
        return pl.ds(pl.multiple_of((px * NY + py) * pair, pair), pair)

    def act_grad_of(b, links):
        totals = [jnp.zeros((top_rows, width), F32) for _ in range(2)]
        for r in [NX - 1] + list(range(NX - 1)):
            for way, buffer in enumerate((ga, gb)):
                links[("ca", "cb")[way]][r].wait_recv()
                left = jnp.concatenate([buffer[b, r, s, k] for s in range(NY) for k in range(NC)], axis=1)
                right = jnp.concatenate(
                    [
                        w_all[b, :, pair_cols(xl[r], yl[s]) if way == 0 else pair_cols(xl[s], yl[r])]
                        for s in range(NY)
                    ],
                    axis=1,
                )
                totals[way] = totals[way] + nt(left, right)
        return jnp.concatenate(totals, axis=0)

    def home_copy(b, r, s):
        return remote(gsend.at[b, r, s], hrecv.at[r, s], gp_send.at[b], home_gp.at[r, s], up)

    def gp_copy(b, r, s, device):
        return remote(gsend.at[b, r, s], crecv.at[b, r, s], gp_send.at[b], gp_recv.at[b, r, s], device)

    def point_grad(b):
        act_t = act[b].astype(F32).T.astype(BF16)
        turn = jnp.where(is_z(b + starts[0]), 2, 0)
        starter = is_z(b + starts[0], b + starts[1])
        device = {"section": jnp.where(is_z(b + starts[0]), zs[0], zs[2])}
        for slot in range(NX):
            r = lax.rem(slot + turn, NX)
            for s in range(NY):
                whole = jnp.concatenate(
                    [
                        jnp.concatenate([ga[b, r, s, k] for k in range(NC)], axis=1),
                        jnp.concatenate([gb[b, s, r, k] for k in range(NC)], axis=1),
                    ],
                    axis=0,
                )
                part = nn(act_t, whole)
                if slot < 2 and b == 0:
                    @pl.when(starter)
                    def _():
                        gsend[b, r, s] = part.astype(BF16)
                        gp_copy(b, r, s, device).start()

                    @pl.when(jnp.logical_not(starter))
                    def _():
                        gpart[b % 2, r, s] = part
                elif slot < 2:
                    @pl.when(z == b)
                    def _():
                        gpart[b % 2, r, s] = part

                    @pl.when(z != b)
                    def _():
                        gsend[b, r, s] = part.astype(BF16)

                    @pl.when(is_z(b + 1))
                    def _():
                        gp_copy(b, r, s, up).start()

                    @pl.when(is_z(b + 2))
                    def _():
                        gp_copy(b, r, s, down).start()

                    @pl.when(is_z(b + 3))
                    def _():
                        home_copy(b, slot, s).start()
                else:
                    gpart[b % 2, r, s] = part

        @pl.when(z == b)
        def _():
            ghome[...] = gpart[b % 2]

    def point_relay(b, way, hop, lo, hi):
        @pl.when(is_z(b + middles[way][hop]))
        def _():
            for j in range(lo, hi):
                r, s = (2 if way == 0 else 0) + j // NY, j % NY
                copy = gp_copy(b, r, s, (up, down)[way])
                copy.wait_recv()
                gsend[b, r, s] = (gpart[b % 2, r, s] + crecv[b, r, s].astype(F32)).astype(BF16)
                copy.start()

    silu_grad(LIVE, act_grad)
    back = (back + input_grad(LIVE)).astype(BF16).astype(F32)
    links = gather_links(LIVE - 1)
    gather_start(LIVE - 1, links, back)
    tsend[...] = nn(top, act[LIVE].astype(F32), HIGH)
    t_sem = lane_of(tsend, z != NZ - 1)
    t_links = [
        remote(tsend, trecv.at[d - 1], t_sem, recv.at[number()], {"section": jnp.int32(NZ - 1)})
        for d in range(1, NZ)
    ]
    for d in range(1, NZ):
        @pl.when(z == (NZ - 1 + d) % NZ)
        def _():
            t_links[d - 1].start()

    gather_second(links)
    conv_weight_grad(LIVE)
    for b in range(LIVE - 1, -1, -1):
        if b + 2 < LIVE:
            point_relay(b + 2, 0, 1, 4, 8)
        if b + 1 < LIVE:
            point_relay(b + 1, 1, 1, 0, 2)
            point_relay(b + 1, 0, 0, 0, 2)
        gather_third(links)
        if b + 1 < LIVE:
            point_relay(b + 1, 1, 1, 2, 6)
            point_relay(b + 1, 0, 0, 2, 6)
        silu_grad(b, act_grad_of(b, links))
        if b > 0:
            back = (back + input_grad(b)).astype(BF16).astype(F32)
            links = gather_links(b - 1)
            gather_start(b - 1, links, back)
        point_grad(b)
        if b + 1 < LIVE:
            point_relay(b + 1, 1, 1, 6, 8)
            point_relay(b + 1, 0, 0, 6, 8)
            point_relay(b + 1, 0, 1, 0, 4)
        if b > 0:
            gather_second(links)
        conv_weight_grad(b)
    point_relay(1, 0, 1, 4, 8)
    for j in range(8):
        for way in range(2):
            point_relay(0, way, 0, j, j + 1)
            if j:
                point_relay(0, way, 1, j - 1, j)
    for way in range(2):
        point_relay(0, way, 1, 7, 8)

    def out_copy(r, s):
        return pltpu.make_async_copy(
            ghome.at[r, s], out_gp.at[0, :, pair_cols(xl[r], yl[s])], out_sem.at[0]
        )

    @pl.when(last)
    def _():
        total = tsend[...]
        for d in range(1, NZ):
            t_links[d - 1].wait_recv()
            total = total + trecv[d - 1]
        total_t = total.T
        for r in range(NX):
            for s in range(NY):
                whole = jnp.concatenate([heads[xl[r], yl[s], k] for k in range(NC)], axis=1)
                ghome[r, s] = nn(total_t, whole, HIGH)
                out_copy(r, s).start()

    for b in range(LIVE):
        @pl.when(z == b)
        def _():
            for j in range(2 * NY):
                for r, s in ((2 + j // NY, j % NY), (j // NY, j % NY)):
                    gp_copy(b, r, s, up).wait_recv()
                    heard = crecv[b, r, s].astype(F32)
                    if b > 0 and r < 2:
                        home_copy(b, r, s).wait_recv()
                        heard = heard + hrecv[r, s].astype(F32)
                    ghome[r, s] = ghome[r, s] + heard
                    out_copy(r, s).start()

    total = gcpart[...]
    for d in range(1, NZ):
        wait_bytes(gccrecv.at[d - 1], home_sems[d - 1])
        total = total + gccrecv[d - 1].astype(F32)
    gcpart[...] = total
    gc_out = pltpu.make_async_copy(gcpart, out_gc.at[0], out_sem.at[1])
    gc_out.start()
    for b in range(LIVE):
        drains.append((gsend.at[b], gp_send.at[b], z != b))
    for ref, sem, when in drains:
        if when is None:
            wait_bytes(ref, sem)
        else:
            pl.when(when)(functools.partial(wait_bytes, ref, sem))
    wait_bytes(ghome, out_sem.at[0])
    gc_out.wait()
    assert sends[0] <= send.shape[0], sends[0]
    assert count[0] <= recv.shape[0], count[0]


def local(inputs, labels, conv_weight, point_weight, head_weight):
    steps, width = inputs.shape[1:]
    blocks, taps, group, _ = conv_weight.shape
    chans = point_weight.shape[2]
    part = steps // 2
    pair = NC * width
    hbm = pl.BlockSpec(memory_space=pl.ANY)
    V = pltpu.VMEM
    dma = pltpu.SemaphoreType.DMA
    scratch = [
        V(labels.shape, labels.dtype),
        V(head_weight.shape, BF16),
        V((8, width), F32),
        V((LIVE, width, chans), BF16),
        V((NZ, taps, group, width), BF16),
        V((width, chans), BF16),
        V((steps, width), BF16),
        V((NZ, taps * width, width), BF16),
        V((NZ, steps, taps * width), BF16),
        V((NZ, steps, width), F32),
        V((NZ, steps, width), BF16),
        V((steps, width), F32),
        V((steps + 16, width), F32),
        V((NZ, steps, width), BF16),
        V((LIVE, NX, NY, part, width), BF16),
        V((LIVE, NX, NY, part, width), BF16),
        V((LIVE, NY, NX, part, width), BF16),
        V((LIVE, NY, NX, part, width), BF16),
        V((LIVE, NX, NY, part, width), BF16),
        V((LIVE, NY, NX, part, width), BF16),
        V((LIVE, NX - 1, NY, part, width), BF16),
        V((LIVE, NY - 1, NX, part, width), BF16),
        V((LIVE, NY - 1, part, width), BF16),
        V((LIVE, NX - 1, part, width), BF16),
        V((LIVE, NY - 1, part, width), BF16),
        V((LIVE, NX - 1, part, width), BF16),
        V((LIVE, NX, NY, NC, part, width), BF16),
        V((LIVE, NY, NX, NC, part, width), BF16),
        V((LIVE, NX, NY, width, pair), BF16),
        V((LIVE, NX, NY, width, pair), BF16),
        V((2, NY, width, pair), BF16),
        V((2, NX, NY, width, pair), F32),
        V((NX, NY, width, pair), F32),
        V((NZ, taps, group, width), BF16),
        V((NZ - 1, taps, group, width), BF16),
        V((taps, group, width), F32),
        V((NX, NY, NC, 8, width), F32),
        V((8, width), F32),
        V((8, width), F32),
        V((NZ - 1, 8, width), F32),
        V((3, 8, steps), F32),
        V((NX + NY - 1, 8, steps), F32),
        dma((80,)),
        dma((222,)),
        dma((LIVE,)),
        dma((LIVE, NX, NY)),
        dma((2, NY)),
        dma((4,)),
        dma((2,)),
    ]
    return pl.pallas_call(
        kernel,
        out_shape=(
            jax.ShapeDtypeStruct(point_weight.shape, F32),
            jax.ShapeDtypeStruct(conv_weight.shape, F32),
        ),
        in_specs=[hbm] * 5,
        out_specs=(hbm, hbm),
        scratch_shapes=scratch,
        compiler_params=pltpu.CompilerParams(
            collective_id=0, has_side_effects=True, vmem_limit_bytes=58 * 1024 * 1024
        ),
    )(inputs, labels, conv_weight, point_weight, head_weight)


def solution(mesh):
    placed = (
        P(None, None, "chan"),
        P(),
        P("section", None, None, "chan"),
        P("section", "chan", None),
        P("chan", None),
    )
    return jax.shard_map(
        local,
        mesh=mesh,
        in_specs=placed,
        out_specs=(P("section", "chan", None), P("section", None, None, "chan")),
        check_vma=False,
    )
```

```python
import functools

import jax
import jax.numpy as jnp
from jax import lax
from jax.experimental import pallas as pl
from jax.experimental.pallas import tpu as pltpu
from jax.sharding import PartitionSpec as P

CLASSES = 3
LOSS_SCALE = 2048
NX, NY, NC, NZ = 4, 4, 2, 4
LIVE = 3
SUB = 4
F32, BF16 = jnp.float32, jnp.bfloat16
HIGH = lax.Precision.HIGHEST
MESH = pl.DeviceIdType.MESH


def nn(a, b, precision=None):
    return lax.dot_general(a, b, (((1,), (0,)), ((), ())), precision=precision, preferred_element_type=F32)


def nt(a, b, precision=None):
    return lax.dot_general(a, b, (((1,), (1,)), ((), ())), precision=precision, preferred_element_type=F32)


def tn(a, b, precision=None):
    return lax.dot_general(a, b, (((0,), (0,)), ((), ())), precision=precision, preferred_element_type=F32)


def wait_bytes(ref, sem):
    pltpu.make_async_copy(ref, ref, sem).wait()


def kernel(
    inputs, labels_in, cw, pw, head_in,
    out_gp, out_gc,
    labels, head_raw, head, w_all, cw_all, w_last, start, dense, cols, conv_out, act, state, pad, cgrad,
    pas, par, pbs, pbr, sa, sb, r1a, r1b, s1a, s1b, r2a, r2b,
    ga, gb, gsend, crecv, hrecv, gpart, ghome, gcsend, gccrecv, gcpart,
    heads, w3h, tsend, trecv, score_own, score_in,
    send, recv, gp_send, gp_recv, home_gp, local_sem, out_sem,
):
    steps, width = start.shape
    taps, group = cw.shape[1], cw.shape[2]
    half = taps // 2
    top_rows = steps // 2
    pair = NC * width
    span = NY * pair
    rows_a, rows_b = pl.ds(0, top_rows), pl.ds(top_rows, top_rows)
    z = lax.axis_index("section")
    me = lax.axis_index("chan")
    c = lax.rem(me, NC)
    y = lax.rem(lax.div(me, NC), NY)
    x = lax.div(me, NC * NY)
    other = 1 - c
    sibling = {"chan": me + 1 - 2 * c}
    xs = [lax.rem(x + 1 + r, NX) for r in range(NX)]
    ys = [lax.rem(y + 1 + r, NY) for r in range(NY)]
    xl = [lax.rem(x + NX - 1 - r, NX) for r in range(NX)]
    yl = [lax.rem(y + NY - 1 - r, NY) for r in range(NY)]
    at_x = [{"chan": (xs[r] * NY + y) * NC + c} for r in range(NX - 1)]
    at_y = [{"chan": (x * NY + ys[r]) * NC + c} for r in range(NY - 1)]
    zs = [lax.rem(z + 1 + r, NZ) for r in range(NZ - 1)]
    up, down = {"section": zs[0]}, {"section": zs[2]}
    last = z == NZ - 1

    def is_z(*places):
        hit = z == places[0] % NZ
        for place in places[1:]:
            hit = hit | (z == place % NZ)
        return hit

    count = [0]

    def number():
        count[0] += 1
        return count[0] - 1

    def remote(src, dst, send_sem, recv_sem, device):
        return pltpu.make_async_remote_copy(
            src_ref=src, dst_ref=dst, send_sem=send_sem, recv_sem=recv_sem,
            device_id=device, device_id_type=MESH,
        )

    sends = [0]
    drains = []

    def lane_of(total, when=None):
        sends[0] += 1
        sem = send.at[sends[0] - 1]
        drains.append((total, sem, when))
        return sem

    def fan(copies, total, when=None):
        sem = lane_of(total, when)
        return [remote(src, dst, sem, recv.at[number()], device) for src, dst, device in copies]

    def link(src, dst, device, when=None):
        return fan([(src, dst, device)], src, when)[0]

    pltpu.make_async_copy(inputs.at[z], start, local_sem.at[0]).start()
    pltpu.make_async_copy(labels_in, labels, local_sem.at[2]).start()
    pltpu.make_async_copy(head_in, head_raw, local_sem.at[3]).start()

    @pl.when(last)
    def _():
        pltpu.make_async_copy(pw.at[0], w_last, local_sem.at[1]).start()

    barrier = pltpu.get_barrier_semaphore()
    peers = [sibling] + at_x + at_y + [{"section": s} for s in zs]
    for peer in peers:
        pl.semaphore_signal(barrier, inc=1, device_id=peer, device_id_type=MESH)
    pl.semaphore_wait(barrier, len(peers))

    class Piece:
        def __init__(self, b, way, src, ref, sem):
            self.src, self.ref, self.sem = src, ref, recv.at[number()]
            device = (up, down)[way]
            self.order = [b + 1, b + 2, b + 3] if way == 0 else [b + 3, b + 2, b + 1]
            self.first = remote(src, ref, sem, self.sem, device)
            self.next = remote(ref, ref, sem, self.sem, device)

        def relay(self, hop):
            @pl.when(is_z(self.order[hop]))
            def _():
                wait_bytes(self.ref, self.sem)
                self.next.start()

        def ready(self):
            @pl.when(jnp.logical_not(is_z(*self.order[:2])))
            def _():
                wait_bytes(self.ref, self.sem)

    taps_of, columns_of = [], []
    for b in range(NZ):
        for way in range(2):
            end = z != (b + (3, 1)[way]) % NZ
            kept = pl.ds(0, half + 1) if way == 0 else pl.ds(half + 1, taps - half - 1)
            ref = cw_all.at[b, kept]
            taps_of.append(Piece(b, way, cw.at[0, kept], ref, lane_of(ref, end)))
            if b < LIVE:
                sem = lane_of(w_all.at[b, :, pl.ds(0, 2 * span)], end)
                pieces = []
                for r in range(way, NX, 2):
                    for k in range(SUB):
                        size = span // SUB
                        at = pl.ds(pl.multiple_of(xs[r] * span + k * size, size), size)
                        pieces.append(Piece(b, way, pw.at[0, :, at], w_all.at[b, :, at], sem))
                columns_of.append(pieces)

    def launch(b, pieces):
        @pl.when(z == b)
        def _():
            for piece in pieces:
                piece.first.start()
            for piece in pieces:
                pltpu.make_async_copy(piece.src, piece.ref, piece.sem).start()

    def both(b):
        return [piece for two in zip(columns_of[2 * b], columns_of[2 * b + 1]) for piece in two]

    def relays(pieces, hop, lo=0, hi=None):
        for piece in pieces[lo:hi]:
            piece.relay(hop)

    head_core = link(heads.at[x, y, c], heads.at[x, y, c], sibling, last)
    head_x = [link(heads.at[x, y], heads.at[x, y], at_x[r], last) for r in range(NX - 1)]
    head_y = [link(heads.at[:, y], heads.at[:, y], at_y[r], last) for r in range(NY - 1)]
    w3h_out = [link(w3h, w3h, {"section": zs[r]}, last) for r in range(NZ - 1)]

    launch(0, taps_of[:2] + both(0))
    for b in range(1, NZ):
        launch(b, taps_of[2 * b : 2 * b + 2])
    launch(1, columns_of[3])

    wait_bytes(labels_in, local_sem.at[2])
    wait_bytes(head_in, local_sem.at[3])
    picked = (
        lax.broadcasted_iota(jnp.int32, (head.shape[0], CLASSES), 0)
        == lax.broadcasted_iota(jnp.int32, (head.shape[0], CLASSES), 1)
    ).astype(F32)
    head[...] = nt(picked, head_raw[...].astype(F32))

    @pl.when(last)
    def _():
        heads[x, y, c] = head[...]
        head_core.start()

    for piece in taps_of[:2] + both(0)[: 2 * SUB]:
        piece.relay(0)
        piece.relay(1)

    @pl.when(last)
    def _():
        head_core.wait_recv()
        for copy in head_x:
            copy.start()

    lane = lax.broadcasted_iota(jnp.int32, (group, width), 1)
    first_group = lane < group
    edge = 8
    pad[pl.ds(0, edge), :] = jnp.zeros((edge, width), F32)
    pad[pl.ds(edge + steps, edge), :] = jnp.zeros((edge, width), F32)
    wait_bytes(start, local_sem.at[0])
    state[...] = start[...].astype(F32)

    def unfold(b):
        pad[pl.ds(edge, steps), :] = state[...]
        for k in range(taps):
            cols[b, :, pl.ds(k * width, width)] = pad[pl.ds(edge + k - half, steps), :].astype(BF16)

    def widen(b):
        for piece in taps_of[2 * b : 2 * b + 2]:
            piece.ready()
        for k in range(taps):
            tap = cw_all[b, k].astype(F32)
            dense[b, pl.ds(k * width, group), :] = jnp.where(first_group, tap, 0.0).astype(BF16)
            dense[b, pl.ds(k * width + group, group), :] = jnp.where(first_group, 0.0, tap).astype(BF16)

    def conv(b):
        value = nn(cols[b], dense[b])
        conv_out[b] = value
        act[b] = (value * jax.nn.sigmoid(value)).astype(BF16)

    unfold(0)
    relays(taps_of[2:], 0)
    for piece in both(0)[2 * SUB : 3 * SUB]:
        piece.relay(0)
        piece.relay(1)

    @pl.when(last)
    def _():
        for copy in head_x:
            copy.wait_recv()
        for copy in head_y:
            copy.start()

    widen(0)
    conv(0)
    for piece in both(0)[3 * SUB :]:
        piece.relay(0)
        piece.relay(1)
    relays(taps_of[2:], 1)

    @pl.when(z == 0)
    def _():
        for piece in columns_of[3]:
            wait_bytes(piece.ref, piece.sem)
        for piece in columns_of[3]:
            piece.next.start()

    launch(1, columns_of[2])
    launch(2, columns_of[5])

    up1, down1, up2, down2 = columns_of[2:6]
    plan = {
        (0, "early"): [(down1, 1, 0, 5), (up1, 0, 0, 2)],
        (0, 1): [(down1, 1, 5, 6), (up1, 0, 2, 3)],
        (0, 2): [(down1, 1, 6, 7), (up1, 0, 3, 4), (up1, 1, 0, 1)],
        (0, 3): [(down1, 1, 7, 8), (up1, 0, 4, 5), (up1, 1, 1, 2)],
        (0, 4): [(up1, 0, 5, 6), (up1, 1, 2, 3), (down2, 0, 0, 1)],
        (0, "sent"): [(up1, 0, 6, 8), (up1, 1, 3, 6), (down2, 0, 1, 4)],
        (0, "middle"): [(up1, 1, 6, 8), (down2, 0, 4, 7)],
        (0, "late"): [(down2, 0, 7, 8)],
        (1, "early"): [(down2, 1, 0, 6), (up2, 0, 0, 1)],
        (1, 1): [(down2, 1, 6, 7), (up2, 0, 1, 2)],
        (1, 2): [(down2, 1, 7, 8), (up2, 0, 2, 3), (up2, 1, 0, 1)],
        (1, 3): [(up2, 0, 3, 4), (up2, 1, 1, 2)],
        (1, "sent"): [(up2, 0, 4, 6), (up2, 1, 2, 4)],
        (1, "middle"): [(up2, 0, 6, 8), (up2, 1, 4, 6)],
        (1, "late"): [(up2, 1, 6, 8)],
    }

    def slot(b, name):
        for pieces, hop, lo, hi in plan.get((b, name), []):
            relays(pieces, hop, lo, hi)
        if (b, name) == (0, "middle"):
            launch(2, up2)

    def mix(b):
        ca = fan([(pas.at[b, r], par.at[b, r], sibling) for r in range(NX)], pas.at[b])
        cb = fan([(pbs.at[b, r], pbr.at[b, r], sibling) for r in range(NY)], pbs.at[b])
        a1 = fan([(sa.at[b, r], r1a.at[b, r], at_x[r]) for r in range(NX - 1)], r1a.at[b])
        b1 = fan([(sb.at[b, r], r1b.at[b, r], at_y[r]) for r in range(NY - 1)], r1b.at[b])
        a2 = fan([(s1a.at[b, r], r2a.at[b, r], at_y[r]) for r in range(NY - 1)], r2a.at[b])
        b2 = fan([(s1b.at[b, r], r2b.at[b, r], at_x[r]) for r in range(NX - 1)], r2b.at[b])

        def weights(place, core):
            return jnp.concatenate(
                [
                    w_all[b, :, pl.ds(pl.multiple_of(place(j) * pair + core * width, width), width)]
                    for j in range(NY)
                ],
                axis=1,
            )

        def line_a(r):
            return lambda j: xs[r] * NY + j

        def line_b(r):
            return lambda i: i * NY + ys[r]

        slot(b, "early")
        for piece in both(b):
            piece.ready()
        for r in range(NX + 1):
            if r < NX:
                for rows, line, out, copy in ((rows_a, line_a, pas, ca), (rows_b, line_b, pbs, cb)):
                    part = nn(act[b, rows, :], weights(line(r), other))
                    for j in range(NY):
                        out[b, r, j] = part[:, j * width : (j + 1) * width].astype(BF16)
                    copy[r].start()
            slot(b, r)
            if r >= 1:
                q = r - 1
                for rows, line, heard, out, copy, first in (
                    (rows_a, line_a, par, sa, ca, a1),
                    (rows_b, line_b, pbr, sb, cb, b1),
                ):
                    part = nn(act[b, rows, :], weights(line(q), c))
                    copy[q].wait_recv()
                    for j in range(NY):
                        out[b, q, j] = (
                            part[:, j * width : (j + 1) * width] + heard[b, q, j].astype(F32)
                        ).astype(BF16)
                    if q < NX - 1:
                        first[q].start()
        slot(b, "sent")
        kept = []
        for first, second, own, heard, out, seen, mine in (
            (a1, a2, sa, r1a, s1a, ys, y),
            (b1, b2, sb, r1b, s1b, xs, x),
        ):
            for copy in first:
                copy.wait_recv()
            if first is b1:
                slot(b, "middle")

            def total_at(j):
                total = own[b, NX - 1, j].astype(F32)
                for q in range(NX - 1):
                    total = total + heard[b, q, j].astype(F32)
                return total

            for r in range(NX - 1):
                out[b, r] = total_at(seen[r]).astype(BF16)
                second[r].start()
            kept.append(total_at(mine))
        slot(b, "late")
        widen(b + 1)
        for rows, second, heard, total in ((rows_a, a2, r2a, kept[0]), (rows_b, b2, r2b, kept[1])):
            for r in range(NX - 1):
                second[r].wait_recv()
                total = total + heard[b, r].astype(F32)
            state[rows, :] = (state[rows, :] + total).astype(BF16).astype(F32)

    for b in range(LIVE):
        if b > 0:
            slot(b - 1, "after")
        if b > 0:
            unfold(b)
            conv(b)
        mix(b)
        if b == 0:
            @pl.when(last)
            def _():
                for copy in head_y:
                    copy.wait_recv()
                wait_bytes(w_last, local_sem.at[1])

                def fold(i, total):
                    whole = jnp.concatenate(
                        [heads[i, j, k] for j in range(NY) for k in range(NC)], axis=1
                    ).astype(BF16)
                    return total + nt(whole, w_last[:, pl.ds(pl.multiple_of(i * span, span), span)])

                w3h[...] = lax.fori_loop(0, NX, fold, jnp.zeros(w3h.shape, F32))
                for copy in w3h_out:
                    copy.start()

    unfold(LIVE)
    conv(LIVE)

    s_core = link(score_own.at[0], score_in.at[0], sibling)
    s_x = [link(score_own.at[1], score_in.at[1 + r], at_x[r]) for r in range(NX - 1)]
    s_y = [link(score_own.at[2], score_in.at[NX + r], at_y[r]) for r in range(NY - 1)]
    for r in range(NZ - 1):
        @pl.when(z == r)
        def _():
            w3h_out[r].wait_recv()

    scores = nt(head[...], state[...], HIGH) + nt(w3h[...], act[LIVE].astype(F32), HIGH)
    score_own[0] = scores
    s_core.start()
    s_core.wait_recv()
    scores = scores + score_in[0]
    score_own[1] = scores
    for copy in s_x:
        copy.start()
    for copy in s_x:
        copy.wait_recv()
    for r in range(NX - 1):
        scores = scores + score_in[1 + r]
    score_own[2] = scores
    for copy in s_y:
        copy.start()
    for copy in s_y:
        copy.wait_recv()
    for r in range(NY - 1):
        scores = scores + score_in[NX + r]
    classes = lax.broadcasted_iota(jnp.int32, scores.shape, 0)
    hot = (classes == labels[pl.ds(z, 1), :]).astype(F32)
    top = (jax.nn.sigmoid(scores) - hot) * (LOSS_SCALE / (NZ * steps))
    top_t = top.T
    back = nn(top_t, head[...], HIGH).astype(BF16).astype(F32)
    act_grad = nn(top_t, w3h[...], HIGH)

    def silu_grad(b, act_grad):
        value = conv_out[b]
        s = jax.nn.sigmoid(value)
        cgrad[b] = (act_grad * s * (1.0 + value * (1.0 - s))).astype(BF16)

    def input_grad(b):
        pad[pl.ds(edge, steps), :] = cgrad[b].astype(F32)
        total = jnp.zeros((steps, width), F32)
        for k in range(taps):
            shifted = pad[pl.ds(edge - k + half, steps), :].astype(BF16)
            total = total + nt(shifted, dense[b, pl.ds(k * width, width), :])
        return total

    starts = [1, 3]
    middles = [(2, 3), (2, 1)]
    home_sems = [recv.at[number()] for _ in range(NZ - 1)]

    def conv_weight_grad(b):
        whole = tn(cols[b], cgrad[b])
        sem = lane_of(gcsend.at[b], z != b)

        def piece(k):
            return jnp.where(
                first_group,
                whole[k * width : k * width + group],
                whole[k * width + group : (k + 1) * width],
            )

        @pl.when(z == b)
        def _():
            for k in range(taps):
                gcpart[k] = piece(k)

        @pl.when(z != b)
        def _():
            for k in range(taps):
                gcsend[b, k] = piece(k).astype(BF16)

        for d in range(1, NZ):
            @pl.when(is_z(b + d))
            def _():
                remote(
                    gcsend.at[b], gccrecv.at[d - 1], sem, home_sems[d - 1], {"section": jnp.int32(b)}
                ).start()

    def gather_links(b):
        own_a, own_b = ga.at[b, NX - 1, NY - 1, c], gb.at[b, NY - 1, NX - 1, c]
        three = r2a.at[0]
        rest = pl.ds(0, NX - 1)
        nine = r1a.at[0, rest, rest]
        line_a, line_b = ga.at[b, NX - 1, rest, c], gb.at[b, NY - 1, rest, c]
        links = {
            "a1": fan([(own_a, ga.at[b, NX - 1, r, c], at_y[r]) for r in range(NY - 1)], three),
            "b1": fan([(own_b, gb.at[b, NY - 1, r, c], at_x[r]) for r in range(NX - 1)], three),
            "a2own": fan([(own_a, ga.at[b, r, NY - 1, c], at_x[r]) for r in range(NX - 1)], three),
            "b2own": fan([(own_b, gb.at[b, r, NX - 1, c], at_y[r]) for r in range(NY - 1)], three),
            "a2": fan([(line_a, ga.at[b, r, rest, c], at_x[r]) for r in range(NX - 1)], nine),
            "b2": fan([(line_b, gb.at[b, r, rest, c], at_y[r]) for r in range(NY - 1)], nine),
            "ca": fan([(ga.at[b, r, :, c], ga.at[b, r, :, c], sibling) for r in range(NX)], pas.at[0]),
            "cb": fan([(gb.at[b, r, :, c], gb.at[b, r, :, c], sibling) for r in range(NY)], pbs.at[0]),
        }
        return links

    def gather_start(b, links, back):
        ga[b, NX - 1, NY - 1, c] = back[:top_rows].astype(BF16)
        gb[b, NY - 1, NX - 1, c] = back[top_rows:].astype(BF16)
        for name in ("a1", "b1", "a2own", "b2own"):
            for copy in links[name]:
                copy.start()

    def gather_second(links):
        for p in "ab":
            for copy in links[p + "1"]:
                copy.wait_recv()
            for copy in links[p + "2"]:
                copy.start()
            links["c" + p][NX - 1].start()

    def gather_third(links):
        for r in range(NX - 1):
            for p in "ab":
                links[p + "2own"][r].wait_recv()
                links[p + "2"][r].wait_recv()
                links["c" + p][r].start()

    def pair_cols(px, py):
        return pl.ds(pl.multiple_of((px * NY + py) * pair, pair), pair)

    def act_grad_of(b, links, waited=False):
        totals = [jnp.zeros((top_rows, width), F32) for _ in range(2)]
        for r in [NX - 1] + list(range(NX - 1)):
            for way, buffer in enumerate((ga, gb)):
                if not waited:
                    links[("ca", "cb")[way]][r].wait_recv()
                left = jnp.concatenate([buffer[b, r, s, k] for s in range(NY) for k in range(NC)], axis=1)
                right = jnp.concatenate(
                    [
                        w_all[b, :, pair_cols(xl[r], yl[s]) if way == 0 else pair_cols(xl[s], yl[r])]
                        for s in range(NY)
                    ],
                    axis=1,
                )
                totals[way] = totals[way] + nt(left, right)
        return jnp.concatenate(totals, axis=0)

    def home_copy(b, r, s):
        return remote(gsend.at[b, r, s], hrecv.at[r, s], gp_send.at[b], home_gp.at[r, s], up)

    def gp_copy(b, r, s, device):
        return remote(gsend.at[b, r, s], crecv.at[b, r, s], gp_send.at[b], gp_recv.at[b, r, s], device)

    def point_grad(b):
        act_t = act[b].astype(F32).T.astype(BF16)
        turn = jnp.where(is_z(b + starts[0]), 2, 0)
        starter = is_z(b + starts[0], b + starts[1])
        device = {"section": jnp.where(is_z(b + starts[0]), zs[0], zs[2])}
        for slot in range(NX):
            r = lax.rem(slot + turn, NX)
            for s in range(NY):
                whole = jnp.concatenate(
                    [
                        jnp.concatenate([ga[b, r, s, k] for k in range(NC)], axis=1),
                        jnp.concatenate([gb[b, s, r, k] for k in range(NC)], axis=1),
                    ],
                    axis=0,
                )
                part = nn(act_t, whole)
                if slot < 2 and b == 0:
                    @pl.when(starter)
                    def _():
                        gsend[b, r, s] = part.astype(BF16)
                        gp_copy(b, r, s, device).start()

                    @pl.when(jnp.logical_not(starter))
                    def _():
                        gpart[b % 2, r, s] = part
                elif slot < 2:
                    @pl.when(z == b)
                    def _():
                        gpart[b % 2, r, s] = part

                    @pl.when(z != b)
                    def _():
                        gsend[b, r, s] = part.astype(BF16)

                    @pl.when(is_z(b + 1))
                    def _():
                        gp_copy(b, r, s, up).start()

                    @pl.when(is_z(b + 2))
                    def _():
                        gp_copy(b, r, s, down).start()

                    @pl.when(is_z(b + 3))
                    def _():
                        home_copy(b, slot, s).start()
                else:
                    gpart[b % 2, r, s] = part

        @pl.when(z == b)
        def _():
            ghome[...] = gpart[b % 2]

    def point_relay(b, way, hop, lo, hi):
        @pl.when(is_z(b + middles[way][hop]))
        def _():
            for j in range(lo, hi):
                r, s = (2 if way == 0 else 0) + j // NY, j % NY
                copy = gp_copy(b, r, s, (up, down)[way])
                copy.wait_recv()
                gsend[b, r, s] = (gpart[b % 2, r, s] + crecv[b, r, s].astype(F32)).astype(BF16)
                copy.start()

    def late_relays(b):
        point_relay(b, 1, 1, 6, 8)
        point_relay(b, 0, 0, 6, 8)
        point_relay(b, 0, 1, 0, 4)

    silu_grad(LIVE, act_grad)
    back = (back + input_grad(LIVE)).astype(BF16).astype(F32)
    links = gather_links(LIVE - 1)
    gather_start(LIVE - 1, links, back)
    tsend[...] = nn(top, act[LIVE].astype(F32), HIGH)
    t_sem = lane_of(tsend, z != NZ - 1)
    t_links = [
        remote(tsend, trecv.at[d - 1], t_sem, recv.at[number()], {"section": jnp.int32(NZ - 1)})
        for d in range(1, NZ)
    ]
    for d in range(1, NZ):
        @pl.when(z == (NZ - 1 + d) % NZ)
        def _():
            t_links[d - 1].start()

    gather_second(links)
    conv_weight_grad(LIVE)
    for b in range(LIVE - 1, -1, -1):
        if b + 2 < LIVE:
            point_relay(b + 2, 0, 1, 4, 8)
        if b + 1 < LIVE:
            point_relay(b + 1, 1, 1, 0, 2)
            point_relay(b + 1, 0, 0, 0, 2)
        gather_third(links)
        if b + 1 < LIVE:
            point_relay(b + 1, 1, 1, 2, 6)
            point_relay(b + 1, 0, 0, 2, 6)
        if b == 0:
            for copy in links["ca"] + links["cb"]:
                copy.wait_recv()
            point_grad(0)
            late_relays(1)
            point_relay(1, 0, 1, 4, 6)
        silu_grad(b, act_grad_of(b, links, b == 0))
        if b > 0:
            back = (back + input_grad(b)).astype(BF16).astype(F32)
            links = gather_links(b - 1)
            gather_start(b - 1, links, back)
            point_grad(b)
            if b + 1 < LIVE:
                late_relays(b + 1)
        if b > 0:
            gather_second(links)
        conv_weight_grad(b)
    point_relay(1, 0, 1, 6, 8)
    for j in range(8):
        for way in range(2):
            point_relay(0, way, 0, j, j + 1)
            if j:
                point_relay(0, way, 1, j - 1, j)
    for way in range(2):
        point_relay(0, way, 1, 7, 8)

    def out_copy(r, s):
        return pltpu.make_async_copy(
            ghome.at[r, s], out_gp.at[0, :, pair_cols(xl[r], yl[s])], out_sem.at[0]
        )

    @pl.when(last)
    def _():
        total = tsend[...]
        for d in range(1, NZ):
            t_links[d - 1].wait_recv()
            total = total + trecv[d - 1]
        total_t = total.T
        for r in range(NX):
            for s in range(NY):
                whole = jnp.concatenate([heads[xl[r], yl[s], k] for k in range(NC)], axis=1)
                ghome[r, s] = nn(total_t, whole, HIGH)
                out_copy(r, s).start()

    for b in range(LIVE):
        @pl.when(z == b)
        def _():
            for j in range(2 * NY):
                for r, s in ((2 + j // NY, j % NY), (j // NY, j % NY)):
                    gp_copy(b, r, s, up).wait_recv()
                    heard = crecv[b, r, s].astype(F32)
                    if b > 0 and r < 2:
                        home_copy(b, r, s).wait_recv()
                        heard = heard + hrecv[r, s].astype(F32)
                    ghome[r, s] = ghome[r, s] + heard
                    out_copy(r, s).start()

    total = gcpart[...]
    for d in range(1, NZ):
        wait_bytes(gccrecv.at[d - 1], home_sems[d - 1])
        total = total + gccrecv[d - 1].astype(F32)
    gcpart[...] = total
    gc_out = pltpu.make_async_copy(gcpart, out_gc.at[0], out_sem.at[1])
    gc_out.start()
    for b in range(LIVE):
        drains.append((gsend.at[b], gp_send.at[b], z != b))
    for ref, sem, when in drains:
        if when is None:
            wait_bytes(ref, sem)
        else:
            pl.when(when)(functools.partial(wait_bytes, ref, sem))
    wait_bytes(ghome, out_sem.at[0])
    gc_out.wait()
    assert sends[0] <= send.shape[0], sends[0]
    assert count[0] <= recv.shape[0], count[0]


def local(inputs, labels, conv_weight, point_weight, head_weight):
    steps, width = inputs.shape[1:]
    blocks, taps, group, _ = conv_weight.shape
    chans = point_weight.shape[2]
    part = steps // 2
    pair = NC * width
    hbm = pl.BlockSpec(memory_space=pl.ANY)
    V = pltpu.VMEM
    dma = pltpu.SemaphoreType.DMA
    scratch = [
        V(labels.shape, labels.dtype),
        V(head_weight.shape, BF16),
        V((8, width), F32),
        V((LIVE, width, chans), BF16),
        V((NZ, taps, group, width), BF16),
        V((width, chans), BF16),
        V((steps, width), BF16),
        V((NZ, taps * width, width), BF16),
        V((NZ, steps, taps * width), BF16),
        V((NZ, steps, width), F32),
        V((NZ, steps, width), BF16),
        V((steps, width), F32),
        V((steps + 16, width), F32),
        V((NZ, steps, width), BF16),
        V((LIVE, NX, NY, part, width), BF16),
        V((LIVE, NX, NY, part, width), BF16),
        V((LIVE, NY, NX, part, width), BF16),
        V((LIVE, NY, NX, part, width), BF16),
        V((LIVE, NX, NY, part, width), BF16),
        V((LIVE, NY, NX, part, width), BF16),
        V((LIVE, NX - 1, NY, part, width), BF16),
        V((LIVE, NY - 1, NX, part, width), BF16),
        V((LIVE, NY - 1, part, width), BF16),
        V((LIVE, NX - 1, part, width), BF16),
        V((LIVE, NY - 1, part, width), BF16),
        V((LIVE, NX - 1, part, width), BF16),
        V((LIVE, NX, NY, NC, part, width), BF16),
        V((LIVE, NY, NX, NC, part, width), BF16),
        V((LIVE, NX, NY, width, pair), BF16),
        V((LIVE, NX, NY, width, pair), BF16),
        V((2, NY, width, pair), BF16),
        V((2, NX, NY, width, pair), F32),
        V((NX, NY, width, pair), F32),
        V((NZ, taps, group, width), BF16),
        V((NZ - 1, taps, group, width), BF16),
        V((taps, group, width), F32),
        V((NX, NY, NC, 8, width), F32),
        V((8, width), F32),
        V((8, width), F32),
        V((NZ - 1, 8, width), F32),
        V((3, 8, steps), F32),
        V((NX + NY - 1, 8, steps), F32),
        dma((80,)),
        dma((222,)),
        dma((LIVE,)),
        dma((LIVE, NX, NY)),
        dma((2, NY)),
        dma((4,)),
        dma((2,)),
    ]
    return pl.pallas_call(
        kernel,
        out_shape=(
            jax.ShapeDtypeStruct(point_weight.shape, F32),
            jax.ShapeDtypeStruct(conv_weight.shape, F32),
        ),
        in_specs=[hbm] * 5,
        out_specs=(hbm, hbm),
        scratch_shapes=scratch,
        compiler_params=pltpu.CompilerParams(
            collective_id=0, has_side_effects=True, vmem_limit_bytes=58 * 1024 * 1024
        ),
    )(inputs, labels, conv_weight, point_weight, head_weight)


def solution(mesh):
    placed = (
        P(None, None, "chan"),
        P(),
        P("section", None, None, "chan"),
        P("section", "chan", None),
        P("chan", None),
    )
    return jax.shard_map(
        local,
        mesh=mesh,
        in_specs=placed,
        out_specs=(P("section", "chan", None), P("section", None, None, "chan")),
        check_vma=False,
    )
```

```python
import functools

import jax
import jax.numpy as jnp
from jax import lax
from jax.experimental import pallas as pl
from jax.experimental.pallas import tpu as pltpu
from jax.sharding import PartitionSpec as P

CLASSES = 3
LOSS_SCALE = 2048
NX, NY, NC, NZ = 4, 4, 2, 4
LIVE = 3
SUB = 4
F32, BF16 = jnp.float32, jnp.bfloat16
HIGH = lax.Precision.HIGHEST
MESH = pl.DeviceIdType.MESH


def nn(a, b, precision=None):
    return lax.dot_general(a, b, (((1,), (0,)), ((), ())), precision=precision, preferred_element_type=F32)


def nt(a, b, precision=None):
    return lax.dot_general(a, b, (((1,), (1,)), ((), ())), precision=precision, preferred_element_type=F32)


def tn(a, b, precision=None):
    return lax.dot_general(a, b, (((0,), (0,)), ((), ())), precision=precision, preferred_element_type=F32)


def wait_bytes(ref, sem):
    pltpu.make_async_copy(ref, ref, sem).wait()


def kernel(
    inputs, labels_in, cw, pw, head_in,
    out_gp, out_gc,
    labels, head_raw, head, w_all, cw_all, w_last, start, dense, cols, conv_out, act, state, pad, cgrad,
    pas, par, pbs, pbr, sa, sb, r1a, r1b, s1a, s1b, r2a, r2b,
    ga, gb, gsend, crecv, hrecv, gpart, ghome, gcsend, gccrecv, gcpart,
    heads, w3h, tsend, trecv, score_own, score_in,
    send, recv, gp_send, gp_recv, home_gp, local_sem, out_sem,
):
    steps, width = start.shape
    taps, group = cw.shape[1], cw.shape[2]
    half = taps // 2
    top_rows = steps // 2
    pair = NC * width
    span = NY * pair
    rows_a, rows_b = pl.ds(0, top_rows), pl.ds(top_rows, top_rows)
    z = lax.axis_index("section")
    me = lax.axis_index("chan")
    c = lax.rem(me, NC)
    y = lax.rem(lax.div(me, NC), NY)
    x = lax.div(me, NC * NY)
    other = 1 - c
    sibling = {"chan": me + 1 - 2 * c}
    xs = [lax.rem(x + 1 + r, NX) for r in range(NX)]
    ys = [lax.rem(y + 1 + r, NY) for r in range(NY)]
    xl = [lax.rem(x + NX - 1 - r, NX) for r in range(NX)]
    yl = [lax.rem(y + NY - 1 - r, NY) for r in range(NY)]
    at_x = [{"chan": (xs[r] * NY + y) * NC + c} for r in range(NX - 1)]
    at_y = [{"chan": (x * NY + ys[r]) * NC + c} for r in range(NY - 1)]
    zs = [lax.rem(z + 1 + r, NZ) for r in range(NZ - 1)]
    up, down = {"section": zs[0]}, {"section": zs[2]}
    last = z == NZ - 1

    def is_z(*places):
        hit = z == places[0] % NZ
        for place in places[1:]:
            hit = hit | (z == place % NZ)
        return hit

    count = [0]

    def number():
        count[0] += 1
        return count[0] - 1

    def remote(src, dst, send_sem, recv_sem, device):
        return pltpu.make_async_remote_copy(
            src_ref=src, dst_ref=dst, send_sem=send_sem, recv_sem=recv_sem,
            device_id=device, device_id_type=MESH,
        )

    sends = [0]
    drains = []

    def lane_of(total, when=None):
        sends[0] += 1
        sem = send.at[sends[0] - 1]
        drains.append((total, sem, when))
        return sem

    def fan(copies, total, when=None):
        sem = lane_of(total, when)
        return [remote(src, dst, sem, recv.at[number()], device) for src, dst, device in copies]

    def link(src, dst, device, when=None):
        return fan([(src, dst, device)], src, when)[0]

    pltpu.make_async_copy(inputs.at[z], start, local_sem.at[0]).start()
    pltpu.make_async_copy(labels_in, labels, local_sem.at[2]).start()
    pltpu.make_async_copy(head_in, head_raw, local_sem.at[3]).start()

    @pl.when(last)
    def _():
        pltpu.make_async_copy(pw.at[0], w_last, local_sem.at[1]).start()

    barrier = pltpu.get_barrier_semaphore()
    peers = [sibling] + at_x + at_y + [{"section": s} for s in zs]
    for peer in peers:
        pl.semaphore_signal(barrier, inc=1, device_id=peer, device_id_type=MESH)
    pl.semaphore_wait(barrier, len(peers))

    class Piece:
        def __init__(self, b, way, src, ref, sem):
            self.src, self.ref, self.sem = src, ref, recv.at[number()]
            device = (up, down)[way]
            self.order = [b + 1, b + 2, b + 3] if way == 0 else [b + 3, b + 2, b + 1]
            self.first = remote(src, ref, sem, self.sem, device)
            self.next = remote(ref, ref, sem, self.sem, device)

        def relay(self, hop):
            @pl.when(is_z(self.order[hop]))
            def _():
                wait_bytes(self.ref, self.sem)
                self.next.start()

        def ready(self):
            @pl.when(jnp.logical_not(is_z(*self.order[:2])))
            def _():
                wait_bytes(self.ref, self.sem)

    taps_of, columns_of = [], []
    for b in range(NZ):
        for way in range(2):
            end = z != (b + (3, 1)[way]) % NZ
            kept = pl.ds(0, half + 1) if way == 0 else pl.ds(half + 1, taps - half - 1)
            ref = cw_all.at[b, kept]
            taps_of.append(Piece(b, way, cw.at[0, kept], ref, lane_of(ref, end)))
            if b < LIVE:
                sem = lane_of(w_all.at[b, :, pl.ds(0, 2 * span)], end)
                pieces = []
                for r in range(way, NX, 2):
                    for k in range(SUB):
                        size = span // SUB
                        at = pl.ds(pl.multiple_of(xs[r] * span + k * size, size), size)
                        pieces.append(Piece(b, way, pw.at[0, :, at], w_all.at[b, :, at], sem))
                columns_of.append(pieces)

    def launch(b, pieces):
        @pl.when(z == b)
        def _():
            for piece in pieces:
                piece.first.start()
            for piece in pieces:
                pltpu.make_async_copy(piece.src, piece.ref, piece.sem).start()

    def both(b):
        return [piece for two in zip(columns_of[2 * b], columns_of[2 * b + 1]) for piece in two]

    def relays(pieces, hop, lo=0, hi=None):
        for piece in pieces[lo:hi]:
            piece.relay(hop)

    head_core = link(heads.at[x, y, c], heads.at[x, y, c], sibling, last)
    head_x = [link(heads.at[x, y], heads.at[x, y], at_x[r], last) for r in range(NX - 1)]
    head_y = [link(heads.at[:, y], heads.at[:, y], at_y[r], last) for r in range(NY - 1)]
    w3h_out = [link(w3h, w3h, {"section": zs[r]}, last) for r in range(NZ - 1)]

    launch(0, taps_of[:2] + both(0))
    for b in range(1, NZ):
        launch(b, taps_of[2 * b : 2 * b + 2])
    launch(1, columns_of[3])

    wait_bytes(labels_in, local_sem.at[2])
    wait_bytes(head_in, local_sem.at[3])
    picked = (
        lax.broadcasted_iota(jnp.int32, (head.shape[0], CLASSES), 0)
        == lax.broadcasted_iota(jnp.int32, (head.shape[0], CLASSES), 1)
    ).astype(F32)
    head[...] = nt(picked, head_raw[...].astype(F32))

    @pl.when(last)
    def _():
        heads[x, y, c] = head[...]
        head_core.start()

    for piece in taps_of[:2] + both(0)[: 2 * SUB]:
        piece.relay(0)
        piece.relay(1)

    @pl.when(last)
    def _():
        head_core.wait_recv()
        for copy in head_x:
            copy.start()

    lane = lax.broadcasted_iota(jnp.int32, (group, width), 1)
    first_group = lane < group
    edge = 8
    pad[pl.ds(0, edge), :] = jnp.zeros((edge, width), F32)
    pad[pl.ds(edge + steps, edge), :] = jnp.zeros((edge, width), F32)
    wait_bytes(start, local_sem.at[0])
    state[...] = start[...].astype(F32)

    def unfold(b):
        pad[pl.ds(edge, steps), :] = state[...]
        for k in range(taps):
            cols[b, :, pl.ds(k * width, width)] = pad[pl.ds(edge + k - half, steps), :].astype(BF16)

    def widen(b):
        for piece in taps_of[2 * b : 2 * b + 2]:
            piece.ready()
        for k in range(taps):
            tap = cw_all[b, k].astype(F32)
            dense[b, pl.ds(k * width, group), :] = jnp.where(first_group, tap, 0.0).astype(BF16)
            dense[b, pl.ds(k * width + group, group), :] = jnp.where(first_group, 0.0, tap).astype(BF16)

    def conv(b):
        value = nn(cols[b], dense[b])
        conv_out[b] = value
        act[b] = (value * jax.nn.sigmoid(value)).astype(BF16)

    unfold(0)
    relays(taps_of[2:], 0)
    for piece in both(0)[2 * SUB : 3 * SUB]:
        piece.relay(0)
        piece.relay(1)

    @pl.when(last)
    def _():
        for copy in head_x:
            copy.wait_recv()
        for copy in head_y:
            copy.start()

    widen(0)
    conv(0)
    for piece in both(0)[3 * SUB :]:
        piece.relay(0)
        piece.relay(1)
    relays(taps_of[2:], 1)

    @pl.when(z == 0)
    def _():
        for piece in columns_of[3]:
            wait_bytes(piece.ref, piece.sem)
        for piece in columns_of[3]:
            piece.next.start()

    launch(1, columns_of[2])
    launch(2, columns_of[5])

    up1, down1, up2, down2 = columns_of[2:6]
    plan = {
        (0, "early"): [(down1, 1, 0, 5), (up1, 0, 0, 2)],
        (0, 1): [(down1, 1, 5, 6), (up1, 0, 2, 3)],
        (0, 2): [(down1, 1, 6, 7), (up1, 0, 3, 4), (up1, 1, 0, 1)],
        (0, 3): [(down1, 1, 7, 8), (up1, 0, 4, 5), (up1, 1, 1, 2)],
        (0, 4): [(up1, 0, 5, 6), (up1, 1, 2, 3), (down2, 0, 0, 1)],
        (0, "sent"): [(up1, 0, 6, 8), (up1, 1, 3, 6), (down2, 0, 1, 4)],
        (0, "middle"): [(up1, 1, 6, 8), (down2, 0, 4, 7)],
        (0, "late"): [(down2, 0, 7, 8)],
        (1, "early"): [(down2, 1, 0, 6), (up2, 0, 0, 1)],
        (1, 1): [(down2, 1, 6, 7), (up2, 0, 1, 2)],
        (1, 2): [(down2, 1, 7, 8), (up2, 0, 2, 3), (up2, 1, 0, 1)],
        (1, 3): [(up2, 0, 3, 4), (up2, 1, 1, 2)],
        (1, "sent"): [(up2, 0, 4, 6), (up2, 1, 2, 4)],
        (1, "middle"): [(up2, 0, 6, 8), (up2, 1, 4, 6)],
        (1, "late"): [(up2, 1, 6, 8)],
    }

    def slot(b, name):
        for pieces, hop, lo, hi in plan.get((b, name), []):
            relays(pieces, hop, lo, hi)
        if (b, name) == (0, "middle"):
            launch(2, up2)

    def mix(b):
        ca = fan([(pas.at[b, r], par.at[b, r], sibling) for r in range(NX)], pas.at[b])
        cb = fan([(pbs.at[b, r], pbr.at[b, r], sibling) for r in range(NY)], pbs.at[b])
        a1 = fan([(sa.at[b, r], r1a.at[b, r], at_x[r]) for r in range(NX - 1)], r1a.at[b])
        b1 = fan([(sb.at[b, r], r1b.at[b, r], at_y[r]) for r in range(NY - 1)], r1b.at[b])
        a2 = fan([(s1a.at[b, r], r2a.at[b, r], at_y[r]) for r in range(NY - 1)], r2a.at[b])
        b2 = fan([(s1b.at[b, r], r2b.at[b, r], at_x[r]) for r in range(NX - 1)], r2b.at[b])

        def weights(place, core):
            return jnp.concatenate(
                [
                    w_all[b, :, pl.ds(pl.multiple_of(place(j) * pair + core * width, width), width)]
                    for j in range(NY)
                ],
                axis=1,
            )

        def line_a(r):
            return lambda j: xs[r] * NY + j

        def line_b(r):
            return lambda i: i * NY + ys[r]

        slot(b, "early")
        for piece in both(b):
            piece.ready()
        for r in range(NX + 1):
            if r < NX:
                for rows, line, out, copy in ((rows_a, line_a, pas, ca), (rows_b, line_b, pbs, cb)):
                    part = nn(act[b, rows, :], weights(line(r), other))
                    for j in range(NY):
                        out[b, r, j] = part[:, j * width : (j + 1) * width].astype(BF16)
                    copy[r].start()
            slot(b, r)
            if r >= 1:
                q = r - 1
                for rows, line, heard, out, copy, first in (
                    (rows_a, line_a, par, sa, ca, a1),
                    (rows_b, line_b, pbr, sb, cb, b1),
                ):
                    part = nn(act[b, rows, :], weights(line(q), c))
                    copy[q].wait_recv()
                    for j in range(NY):
                        out[b, q, j] = (
                            part[:, j * width : (j + 1) * width] + heard[b, q, j].astype(F32)
                        ).astype(BF16)
                    if q < NX - 1:
                        first[q].start()
        slot(b, "sent")
        kept = []
        for first, second, own, heard, out, seen, mine in (
            (a1, a2, sa, r1a, s1a, ys, y),
            (b1, b2, sb, r1b, s1b, xs, x),
        ):
            for copy in first:
                copy.wait_recv()
            if first is b1:
                slot(b, "middle")

            def total_at(j):
                total = own[b, NX - 1, j].astype(F32)
                for q in range(NX - 1):
                    total = total + heard[b, q, j].astype(F32)
                return total

            for r in range(NX - 1):
                out[b, r] = total_at(seen[r]).astype(BF16)
                second[r].start()
            kept.append(total_at(mine))
        slot(b, "late")
        widen(b + 1)
        for rows, second, heard, total in ((rows_a, a2, r2a, kept[0]), (rows_b, b2, r2b, kept[1])):
            for r in range(NX - 1):
                second[r].wait_recv()
                total = total + heard[b, r].astype(F32)
            state[rows, :] = (state[rows, :] + total).astype(BF16).astype(F32)

    for b in range(LIVE):
        if b > 0:
            slot(b - 1, "after")
        if b > 0:
            unfold(b)
            conv(b)
        mix(b)
        if b == 0:
            @pl.when(last)
            def _():
                for copy in head_y:
                    copy.wait_recv()
                wait_bytes(w_last, local_sem.at[1])

                def fold(i, total):
                    whole = jnp.concatenate(
                        [heads[i, j, k] for j in range(NY) for k in range(NC)], axis=1
                    ).astype(BF16)
                    return total + nt(whole, w_last[:, pl.ds(pl.multiple_of(i * span, span), span)])

                w3h[...] = lax.fori_loop(0, NX, fold, jnp.zeros(w3h.shape, F32))
                for copy in w3h_out:
                    copy.start()

    unfold(LIVE)
    conv(LIVE)

    s_core = link(score_own.at[0], score_in.at[0], sibling)
    s_x = [link(score_own.at[1], score_in.at[1 + r], at_x[r]) for r in range(NX - 1)]
    s_y = [link(score_own.at[2], score_in.at[NX + r], at_y[r]) for r in range(NY - 1)]
    for r in range(NZ - 1):
        @pl.when(z == r)
        def _():
            w3h_out[r].wait_recv()

    scores = nt(head[...], state[...], HIGH) + nt(w3h[...], act[LIVE].astype(F32), HIGH)
    score_own[0] = scores
    s_core.start()
    s_core.wait_recv()
    scores = scores + score_in[0]
    score_own[1] = scores
    for copy in s_x:
        copy.start()
    for copy in s_x:
        copy.wait_recv()
    for r in range(NX - 1):
        scores = scores + score_in[1 + r]
    score_own[2] = scores
    for copy in s_y:
        copy.start()
    for copy in s_y:
        copy.wait_recv()
    for r in range(NY - 1):
        scores = scores + score_in[NX + r]
    classes = lax.broadcasted_iota(jnp.int32, scores.shape, 0)
    hot = (classes == labels[pl.ds(z, 1), :]).astype(F32)
    top = (jax.nn.sigmoid(scores) - hot) * (LOSS_SCALE / (NZ * steps))
    top_t = top.T
    back = nn(top_t, head[...], HIGH).astype(BF16).astype(F32)
    act_grad = nn(top_t, w3h[...], HIGH)

    def silu_grad(b, act_grad):
        value = conv_out[b]
        s = jax.nn.sigmoid(value)
        cgrad[b] = (act_grad * s * (1.0 + value * (1.0 - s))).astype(BF16)

    def input_grad(b):
        pad[pl.ds(edge, steps), :] = cgrad[b].astype(F32)
        total = jnp.zeros((steps, width), F32)
        for k in range(taps):
            shifted = pad[pl.ds(edge - k + half, steps), :].astype(BF16)
            total = total + nt(shifted, dense[b, pl.ds(k * width, width), :])
        return total

    starts = [1, 3]
    middles = [(2, 3), (2, 1)]
    home_sems = [recv.at[number()] for _ in range(NZ - 1)]

    def conv_weight_grad(b):
        whole = tn(cols[b], cgrad[b])
        sem = lane_of(gcsend.at[b], z != b)

        def piece(k):
            return jnp.where(
                first_group,
                whole[k * width : k * width + group],
                whole[k * width + group : (k + 1) * width],
            )

        @pl.when(z == b)
        def _():
            for k in range(taps):
                gcpart[k] = piece(k)

        @pl.when(z != b)
        def _():
            for k in range(taps):
                gcsend[b, k] = piece(k).astype(BF16)

        for d in range(1, NZ):
            @pl.when(is_z(b + d))
            def _():
                remote(
                    gcsend.at[b], gccrecv.at[d - 1], sem, home_sems[d - 1], {"section": jnp.int32(b)}
                ).start()

    def gather_links(b):
        own_a, own_b = ga.at[b, NX - 1, NY - 1, c], gb.at[b, NY - 1, NX - 1, c]
        three = r2a.at[0]
        rest = pl.ds(0, NX - 1)
        nine = r1a.at[0, rest, rest]
        line_a, line_b = ga.at[b, NX - 1, rest, c], gb.at[b, NY - 1, rest, c]
        links = {
            "a1": fan([(own_a, ga.at[b, NX - 1, r, c], at_y[r]) for r in range(NY - 1)], three),
            "b1": fan([(own_b, gb.at[b, NY - 1, r, c], at_x[r]) for r in range(NX - 1)], three),
            "a2own": fan([(own_a, ga.at[b, r, NY - 1, c], at_x[r]) for r in range(NX - 1)], three),
            "b2own": fan([(own_b, gb.at[b, r, NX - 1, c], at_y[r]) for r in range(NY - 1)], three),
            "a2": fan([(line_a, ga.at[b, r, rest, c], at_x[r]) for r in range(NX - 1)], nine),
            "b2": fan([(line_b, gb.at[b, r, rest, c], at_y[r]) for r in range(NY - 1)], nine),
            "ca": fan([(ga.at[b, r, :, c], ga.at[b, r, :, c], sibling) for r in range(NX)], pas.at[0]),
            "cb": fan([(gb.at[b, r, :, c], gb.at[b, r, :, c], sibling) for r in range(NY)], pbs.at[0]),
        }
        return links

    def gather_start(b, links, back):
        ga[b, NX - 1, NY - 1, c] = back[:top_rows].astype(BF16)
        gb[b, NY - 1, NX - 1, c] = back[top_rows:].astype(BF16)
        for name in ("a1", "b1", "a2own", "b2own"):
            for copy in links[name]:
                copy.start()

    def gather_second(links):
        for p in "ab":
            for copy in links[p + "1"]:
                copy.wait_recv()
            for copy in links[p + "2"]:
                copy.start()
            links["c" + p][NX - 1].start()

    def gather_third(links):
        for r in range(NX - 1):
            for p in "ab":
                links[p + "2own"][r].wait_recv()
                links[p + "2"][r].wait_recv()
                links["c" + p][r].start()

    def pair_cols(px, py):
        return pl.ds(pl.multiple_of((px * NY + py) * pair, pair), pair)

    def act_grad_of(b, links, waited=False):
        totals = [jnp.zeros((top_rows, width), F32) for _ in range(2)]
        for r in [NX - 1] + list(range(NX - 1)):
            for way, buffer in enumerate((ga, gb)):
                if not waited:
                    links[("ca", "cb")[way]][r].wait_recv()
                left = jnp.concatenate([buffer[b, r, s, k] for s in range(NY) for k in range(NC)], axis=1)
                right = jnp.concatenate(
                    [
                        w_all[b, :, pair_cols(xl[r], yl[s]) if way == 0 else pair_cols(xl[s], yl[r])]
                        for s in range(NY)
                    ],
                    axis=1,
                )
                totals[way] = totals[way] + nt(left, right)
        return jnp.concatenate(totals, axis=0)

    def home_copy(b, r, s):
        return remote(gsend.at[b, r, s], hrecv.at[r, s], gp_send.at[b], home_gp.at[r, s], up)

    def gp_copy(b, r, s, device):
        return remote(gsend.at[b, r, s], crecv.at[b, r, s], gp_send.at[b], gp_recv.at[b, r, s], device)

    def point_grad(b):
        act_t = act[b].astype(F32).T.astype(BF16)
        turn = jnp.where(is_z(b + starts[0]), 2, 0)
        starter = is_z(b + starts[0], b + starts[1])
        device = {"section": jnp.where(is_z(b + starts[0]), zs[0], zs[2])}
        for slot in range(NX):
            r = lax.rem(slot + turn, NX)
            for s in range(NY):
                whole = jnp.concatenate(
                    [
                        jnp.concatenate([ga[b, r, s, k] for k in range(NC)], axis=1),
                        jnp.concatenate([gb[b, s, r, k] for k in range(NC)], axis=1),
                    ],
                    axis=0,
                )
                part = nn(act_t, whole)
                if slot < 2 and b == 0:
                    @pl.when(starter)
                    def _():
                        gsend[b, r, s] = part.astype(BF16)
                        gp_copy(b, r, s, device).start()

                    @pl.when(jnp.logical_not(starter))
                    def _():
                        gpart[b % 2, r, s] = part
                elif slot < 2:
                    @pl.when(z == b)
                    def _():
                        gpart[b % 2, r, s] = part

                    @pl.when(z != b)
                    def _():
                        gsend[b, r, s] = part.astype(BF16)

                    @pl.when(is_z(b + 1))
                    def _():
                        gp_copy(b, r, s, up).start()

                    @pl.when(is_z(b + 2))
                    def _():
                        gp_copy(b, r, s, down).start()

                    @pl.when(is_z(b + 3))
                    def _():
                        home_copy(b, slot, s).start()
                else:
                    gpart[b % 2, r, s] = part

        @pl.when(z == b)
        def _():
            ghome[...] = gpart[b % 2]

    def point_relay(b, way, hop, lo, hi):
        @pl.when(is_z(b + middles[way][hop]))
        def _():
            for j in range(lo, hi):
                r, s = (2 if way == 0 else 0) + j // NY, j % NY
                copy = gp_copy(b, r, s, (up, down)[way])
                copy.wait_recv()
                gsend[b, r, s] = (gpart[b % 2, r, s] + crecv[b, r, s].astype(F32)).astype(BF16)
                copy.start()

    def late_relays(b):
        point_relay(b, 1, 1, 7, 8)
        point_relay(b, 0, 0, 7, 8)
        point_relay(b, 0, 1, 2, 4)

    silu_grad(LIVE, act_grad)
    back = (back + input_grad(LIVE)).astype(BF16).astype(F32)
    links = gather_links(LIVE - 1)
    gather_start(LIVE - 1, links, back)
    tsend[...] = nn(top, act[LIVE].astype(F32), HIGH)
    t_sem = lane_of(tsend, z != NZ - 1)
    t_links = [
        remote(tsend, trecv.at[d - 1], t_sem, recv.at[number()], {"section": jnp.int32(NZ - 1)})
        for d in range(1, NZ)
    ]
    for d in range(1, NZ):
        @pl.when(z == (NZ - 1 + d) % NZ)
        def _():
            t_links[d - 1].start()

    gather_second(links)
    conv_weight_grad(LIVE)
    for b in range(LIVE - 1, -1, -1):
        if b + 2 < LIVE:
            point_relay(b + 2, 0, 1, 4, 8)
        if b + 1 < LIVE:
            point_relay(b + 1, 1, 1, 0, 3)
            point_relay(b + 1, 0, 0, 0, 3)
        gather_third(links)
        if b + 1 < LIVE:
            point_relay(b + 1, 1, 1, 3, 7)
            point_relay(b + 1, 0, 0, 3, 7)
            point_relay(b + 1, 0, 1, 0, 2)
        if b == 0:
            for copy in links["ca"] + links["cb"]:
                copy.wait_recv()
            point_grad(0)
            late_relays(1)
            point_relay(1, 0, 1, 4, 6)
        silu_grad(b, act_grad_of(b, links, b == 0))
        if b > 0:
            back = (back + input_grad(b)).astype(BF16).astype(F32)
            links = gather_links(b - 1)
            gather_start(b - 1, links, back)
            point_grad(b)
            if b + 1 < LIVE:
                late_relays(b + 1)
        if b > 0:
            gather_second(links)
        conv_weight_grad(b)
    point_relay(1, 0, 1, 6, 8)
    for j in range(8):
        for way in range(2):
            point_relay(0, way, 0, j, j + 1)
            if j:
                point_relay(0, way, 1, j - 1, j)
    for way in range(2):
        point_relay(0, way, 1, 7, 8)

    def out_copy(r, s):
        return pltpu.make_async_copy(
            ghome.at[r, s], out_gp.at[0, :, pair_cols(xl[r], yl[s])], out_sem.at[0]
        )

    @pl.when(last)
    def _():
        total = tsend[...]
        for d in range(1, NZ):
            t_links[d - 1].wait_recv()
            total = total + trecv[d - 1]
        total_t = total.T
        for r in range(NX):
            for s in range(NY):
                whole = jnp.concatenate([heads[xl[r], yl[s], k] for k in range(NC)], axis=1)
                ghome[r, s] = nn(total_t, whole, HIGH)
                out_copy(r, s).start()

    for b in range(LIVE):
        @pl.when(z == b)
        def _():
            for j in range(2 * NY):
                for r, s in ((2 + j // NY, j % NY), (j // NY, j % NY)):
                    gp_copy(b, r, s, up).wait_recv()
                    heard = crecv[b, r, s].astype(F32)
                    if b > 0 and r < 2:
                        home_copy(b, r, s).wait_recv()
                        heard = heard + hrecv[r, s].astype(F32)
                    ghome[r, s] = ghome[r, s] + heard
                    out_copy(r, s).start()

    total = gcpart[...]
    for d in range(1, NZ):
        wait_bytes(gccrecv.at[d - 1], home_sems[d - 1])
        total = total + gccrecv[d - 1].astype(F32)
    gcpart[...] = total
    gc_out = pltpu.make_async_copy(gcpart, out_gc.at[0], out_sem.at[1])
    gc_out.start()
    for b in range(LIVE):
        drains.append((gsend.at[b], gp_send.at[b], z != b))
    for ref, sem, when in drains:
        if when is None:
            wait_bytes(ref, sem)
        else:
            pl.when(when)(functools.partial(wait_bytes, ref, sem))
    wait_bytes(ghome, out_sem.at[0])
    gc_out.wait()
    assert sends[0] <= send.shape[0], sends[0]
    assert count[0] <= recv.shape[0], count[0]


def local(inputs, labels, conv_weight, point_weight, head_weight):
    steps, width = inputs.shape[1:]
    blocks, taps, group, _ = conv_weight.shape
    chans = point_weight.shape[2]
    part = steps // 2
    pair = NC * width
    hbm = pl.BlockSpec(memory_space=pl.ANY)
    V = pltpu.VMEM
    dma = pltpu.SemaphoreType.DMA
    scratch = [
        V(labels.shape, labels.dtype),
        V(head_weight.shape, BF16),
        V((8, width), F32),
        V((LIVE, width, chans), BF16),
        V((NZ, taps, group, width), BF16),
        V((width, chans), BF16),
        V((steps, width), BF16),
        V((NZ, taps * width, width), BF16),
        V((NZ, steps, taps * width), BF16),
        V((NZ, steps, width), F32),
        V((NZ, steps, width), BF16),
        V((steps, width), F32),
        V((steps + 16, width), F32),
        V((NZ, steps, width), BF16),
        V((LIVE, NX, NY, part, width), BF16),
        V((LIVE, NX, NY, part, width), BF16),
        V((LIVE, NY, NX, part, width), BF16),
        V((LIVE, NY, NX, part, width), BF16),
        V((LIVE, NX, NY, part, width), BF16),
        V((LIVE, NY, NX, part, width), BF16),
        V((LIVE, NX - 1, NY, part, width), BF16),
        V((LIVE, NY - 1, NX, part, width), BF16),
        V((LIVE, NY - 1, part, width), BF16),
        V((LIVE, NX - 1, part, width), BF16),
        V((LIVE, NY - 1, part, width), BF16),
        V((LIVE, NX - 1, part, width), BF16),
        V((LIVE, NX, NY, NC, part, width), BF16),
        V((LIVE, NY, NX, NC, part, width), BF16),
        V((LIVE, NX, NY, width, pair), BF16),
        V((LIVE, NX, NY, width, pair), BF16),
        V((2, NY, width, pair), BF16),
        V((2, NX, NY, width, pair), F32),
        V((NX, NY, width, pair), F32),
        V((NZ, taps, group, width), BF16),
        V((NZ - 1, taps, group, width), BF16),
        V((taps, group, width), F32),
        V((NX, NY, NC, 8, width), F32),
        V((8, width), F32),
        V((8, width), F32),
        V((NZ - 1, 8, width), F32),
        V((3, 8, steps), F32),
        V((NX + NY - 1, 8, steps), F32),
        dma((80,)),
        dma((222,)),
        dma((LIVE,)),
        dma((LIVE, NX, NY)),
        dma((2, NY)),
        dma((4,)),
        dma((2,)),
    ]
    return pl.pallas_call(
        kernel,
        out_shape=(
            jax.ShapeDtypeStruct(point_weight.shape, F32),
            jax.ShapeDtypeStruct(conv_weight.shape, F32),
        ),
        in_specs=[hbm] * 5,
        out_specs=(hbm, hbm),
        scratch_shapes=scratch,
        compiler_params=pltpu.CompilerParams(
            collective_id=0, has_side_effects=True, vmem_limit_bytes=58 * 1024 * 1024
        ),
    )(inputs, labels, conv_weight, point_weight, head_weight)


def solution(mesh):
    placed = (
        P(None, None, "chan"),
        P(),
        P("section", None, None, "chan"),
        P("section", "chan", None),
        P("chan", None),
    )
    return jax.shard_map(
        local,
        mesh=mesh,
        in_specs=placed,
        out_specs=(P("section", "chan", None), P("section", None, None, "chan")),
        check_vma=False,
    )
```
